128 devices in a mesh: rows: 32 (over x, y, core), rep: 4 (over z).
Axes of the slice: x: 4, y: 4, z: 4, core: 2. Of those that a mesh axis runs over, the one named last changes fastest.
Arguments:
- features: float32 [32768, 602], P(('rows', 'rep')), may hold values from -6 to 6
- weight: float32 [602, 512], replicated, may hold values from -0.25 to 0.25
- cotangent: float32 [32768, 512], P(('rows', 'rep')), may hold values from -4 to 4
- tile_values: float32 [4096, 128, 128], P(('rows', 'rep')), may hold values from -0.1875 to 0.1875
- tile_row: int32 [4096], P(('rows', 'rep')), may hold values from 0 to 7
- tile_col: int32 [4096], P(('rows', 'rep')), may hold values from 0 to 63
- tile_count: int32 [128], P(('rows', 'rep')), may hold values from 8 to 32, as said below
Outputs:
- activated: float32 [32768, 512], P(('rows', 'rep'))
- grad_features: float32 [32768, 602], P(('rows', 'rep'))
- grad_weight: float32 [602, 512], replicated
The draws below stay inside these ranges and needn't reach their ends.
Inputs may be any that keep to these rules, and one draw needn't show every extreme that they name: `tile_count`: slots at or beyond a device's count hold no tile; some device has all 32 slots live.
All inputs are finite; a program needn't handle non-finite values.
Results may differ from the reference program's by a relative error of at most 0.0003.
Values sent between devices are 32-bit elements; how exact they have to be, the bound alone decides.
A program may use at most 128 MiB of HBM per device.

```python
import jax
import jax.numpy as jnp
from jax import lax

F_IN = 602
HID = 512
BLOCK = 128
BLK_DEV = 2
TILE_CAP = 32
NODES = 32768
TILES = 4096
N_ROWS = 32
N_REP = 4


def draw_tile_count(key, part):
    key = jax.random.fold_in(key, 7)
    first_key, second_key = jax.random.split(key)
    counts = jax.random.randint(first_key, (N_ROWS * N_REP,), TILE_CAP // 4, TILE_CAP + 1)
    busiest = jax.random.randint(second_key, (), 0, N_ROWS * N_REP)
    return counts.at[busiest].set(TILE_CAP).astype(jnp.int32)


def with_ends(values, key, least, largest):
    longest = values.shape.index(max(values.shape))
    spots = []
    for shift in (0, 1):
        where = [jax.random.randint(jax.random.fold_in(key, axis), (), 0, length) for axis, length in enumerate(values.shape)]
        where[longest] = (where[longest] + shift) % values.shape[longest]
        spots.append(tuple(where))
    return values.at[spots[0]].set(least).at[spots[1]].set(largest)


def block_scale(rng, dims, cuts, low, high):
    gain = 1.0
    for position, shards_of in cuts:
        steps = jax.random.uniform(jax.random.fold_in(jax.random.fold_in(rng, 6), position), (shards_of,), jnp.float32, low / len(cuts), high / len(cuts))
        gain = gain * jnp.repeat(jnp.exp(steps), dims[position] // shards_of).reshape((-1,) + (1,) * (len(dims) - 1 - position))
    return gain


def noise(key, dims, spread, bound, pieces=(), held_as=jnp.bfloat16):
    values = jax.random.normal(key, dims, jnp.float32) * spread
    if len(pieces) > 0:
        values = block_scale(key, dims, pieces, -0.22, 0.18) * values
    return jnp.clip(values, min=-bound, max=bound).astype(held_as)


def setup_inputs(seed: int = 0) -> dict:
    splits = jax.random.split(jax.random.key(seed), 8)
    features = noise(splits[0], (NODES, F_IN), 1.0, 6.0, ((0, 128),), jnp.float32)
    weight = noise(splits[1], (F_IN, HID), F_IN ** -0.5, 0.25, (), jnp.float32)
    cotangent = noise(splits[2], (NODES, HID), 0.25, 4.0, ((0, 128),), jnp.float32)
    tile_values = noise(splits[3], (TILES, BLOCK, BLOCK), (TILE_CAP * BLOCK // (2 * BLK_DEV)) ** -0.5, 0.1875, ((0, 128),), jnp.float32)
    tile_row = with_ends(jax.random.randint(splits[4], (TILES,), 0, N_REP * BLK_DEV), jax.random.fold_in(splits[4], 1), 0, (N_REP * BLK_DEV) - 1).astype(jnp.int32)
    tile_col = with_ends(jax.random.randint(splits[5], (TILES,), 0, N_ROWS * BLK_DEV), jax.random.fold_in(splits[5], 1), 0, (N_ROWS * BLK_DEV) - 1).astype(jnp.int32)
    tile_count = draw_tile_count(jax.random.fold_in(splits[7], 71), 0)
    return {"features": features, "weight": weight, "cotangent": cotangent, "tile_values": tile_values, "tile_row": tile_row, "tile_col": tile_col, "tile_count": tile_count}


def placed(device, row_idx, col_idx):
    row_dev = device // N_REP
    rep_dev = device % N_REP
    global_row = (row_dev * N_REP * BLK_DEV + row_idx).astype(jnp.int32)
    global_col = (((col_idx // BLK_DEV) * N_REP + rep_dev) * BLK_DEV + col_idx % BLK_DEV).astype(jnp.int32)
    return global_row, global_col


def reference(features, weight, cotangent, tile_values, tile_row, tile_col, tile_count):
    highest = lax.Precision.HIGHEST
    devices = N_ROWS * N_REP
    total_blocks = NODES // BLOCK
    projected = jnp.dot(features, weight, precision=highest, preferred_element_type=jnp.float32)
    blocks = projected.reshape(total_blocks, BLOCK, HID)
    values = tile_values.reshape(devices, TILE_CAP, BLOCK, BLOCK)
    row_local = tile_row.reshape(devices, TILE_CAP)
    col_local = tile_col.reshape(devices, TILE_CAP)
    slots = jnp.arange(TILE_CAP, dtype=jnp.int32)
    device_ids = jnp.arange(devices, dtype=jnp.int32)
    items = (device_ids, values, row_local, col_local, tile_count)

    def forward_step(total, item):
        device, tiles, row_idx, col_idx, live = item
        global_row, global_col = placed(device, row_idx, col_idx)
        alive = (slots < live).astype(jnp.float32)
        product = jnp.einsum("tij,tjh->tih", tiles, blocks[global_col], precision=highest) * alive[:, None, None]
        return total.at[global_row].add(product), None

    summed, _ = lax.scan(forward_step, jnp.zeros((total_blocks, BLOCK, HID), jnp.float32), items)
    summed = summed.reshape(NODES, HID)
    sigma = jax.nn.sigmoid(summed)
    activated = summed * sigma
    grad_pre = cotangent * sigma * (1.0 + summed * (1.0 - sigma))
    grad_blocks = grad_pre.reshape(total_blocks, BLOCK, HID)

    def backward_step(total, item):
        device, tiles, row_idx, col_idx, live = item
        global_row, global_col = placed(device, row_idx, col_idx)
        alive = (slots < live).astype(jnp.float32)
        product = jnp.einsum("tij,tih->tjh", tiles, grad_blocks[global_row], precision=highest) * alive[:, None, None]
        return total.at[global_col].add(product), None

    propagated, _ = lax.scan(backward_step, jnp.zeros((total_blocks, BLOCK, HID), jnp.float32), items)
    propagated = propagated.reshape(NODES, HID)
    grad_weight = jnp.dot(features.T, propagated, precision=highest, preferred_element_type=jnp.float32)
    grad_features = jnp.dot(propagated, weight.T, precision=highest, preferred_element_type=jnp.float32)
    return activated, grad_features, grad_weight
```

```python
import functools

import jax
import jax.numpy as jnp
from jax import lax
from jax.experimental import pallas as pl
from jax.experimental.pallas import tpu as pltpu
from jax.sharding import PartitionSpec as P

MESH = pl.DeviceIdType.MESH
F32 = jnp.float32
BF16 = jnp.bfloat16

BLOCK = 128
HALF = BLOCK // 2
SLOTS = 32
CHUNKS = 4
SIDE = 4
PAD = 640
COPIES = 69 * CHUNKS

ROWS, COLS = 8, 64
ROW_PREV, ROW_LAST, COL_PREV, COL_LAST = 0, SLOTS, SLOTS + ROWS, 2 * SLOTS + ROWS

LO, HI = pl.ds(0, HALF), pl.ds(HALF, HALF)


def split(value):
    high = value.astype(BF16)
    return high, (value - high.astype(F32)).astype(BF16)


def mm(a, b):
    left = jnp.concatenate([a[0], a[1], a[0]], axis=1)
    right = jnp.concatenate([b[0], b[0], b[1]], axis=0)
    return jnp.dot(left, right, preferred_element_type=F32)


def mm_nt(a, b):
    left = jnp.concatenate([a[0], a[1], a[0]], axis=1)
    right = jnp.concatenate([b[0], b[0], b[1]], axis=1)
    return lax.dot_general(left, right, (((1,), (1,)), ((), ())), preferred_element_type=F32)


def kernel(*refs):
    C = CHUNKS
    row_ref, col_ref, live_ref, f_hbm, w_hbm, cot_hbm, tiles_hbm, act_ref, gf_ref, gw_ref = refs[:10]
    refs = list(refs[10:])

    def take(count):
        out = refs[:count]
        del refs[:count]
        return out

    G, R0, part, zfin, GG = (take(C) for _ in range(5))
    m1, f1, m2, f2 = (take(C) for _ in range(4))
    gwl, sb, zb, xb, yb, gwo = (take(C) for _ in range(6))
    slots, tiles, tiles_t, w_raw, w_pad, f_raw, cot, f_hi, f_lo, ft_hi, ft_lo, prop, gf_acc, plan = take(14)
    send_sem, recv_sem, load_sem = take(3)
    W = prop.shape[1] // C

    r = lax.axis_index("rows")
    z = lax.axis_index("rep")
    x, y, p = r // 8, (r // 2) % 4, r % 2
    q = 1 - p

    def at(i, d):
        return (i + d) % SIDE

    def dev(dx=0, dy=0, dz=0, core=None):
        c = p if core is None else core
        return (at(x, dx) * 8 + at(y, dy) * 2 + c, at(z, dz))

    xl, xr, xo = at(x, 3), at(x, 1), at(x, 2)
    yl, yr, yo = at(y, 3), at(y, 1), at(y, 2)
    zl, zr, zo = at(z, 3), at(z, 1), at(z, 2)
    XR, XL, YR, YL, ZR, ZL = dev(dx=1), dev(dx=3), dev(dy=1), dev(dy=3), dev(dz=1), dev(dz=3)
    SIB = dev(core=q)

    count = [0]
    sent = []

    def send(src, dst, device):
        i = count[0]
        count[0] += 1
        copy = pltpu.make_async_remote_copy(
            src_ref=src, dst_ref=dst, send_sem=send_sem.at[i], recv_sem=recv_sem.at[i],
            device_id=device, device_id_type=MESH)
        copy.start()
        sent.append(copy)
        return copy

    def arrive(copies):
        for copy in copies:
            copy.wait_recv()

    def left(copies):
        for copy in copies:
            copy.wait_send()
            sent[:] = [other for other in sent if other is not copy]

    loads = [
        pltpu.make_async_copy(src, dst, load_sem.at[i])
        for i, (src, dst) in enumerate(((f_hbm, f_raw), (w_hbm, w_raw), (cot_hbm, cot), (tiles_hbm, tiles)))
    ]
    for load in loads:
        load.start()
    load_f, load_w, load_cot, load_tiles = loads

    barrier = pltpu.get_barrier_semaphore()
    peers = [dev(dx=d) for d in (1, 2, 3)] + [dev(dy=d) for d in (1, 2, 3)] + [dev(dz=d) for d in (1, 2, 3)] + [SIB]
    for peer in peers:
        pl.semaphore_signal(barrier, inc=1, device_id=peer, device_id_type=MESH)

    F_IN = f_hbm.shape[0]
    tail = F_IN // 8 * 8
    ft_pad = gf_acc
    load_f.wait()
    ft_pad[pl.ds(tail, PAD - tail), :] = jnp.zeros((PAD - tail, ft_pad.shape[1]), F32)
    ft_pad[pl.ds(0, F_IN), :] = f_raw[...]
    f_hi[...], f_lo[...] = split(ft_pad[...].T)
    load_w.wait()
    w_pad[pl.ds(tail, PAD - tail), :] = jnp.zeros((PAD - tail, w_pad.shape[1]), F32)
    w_pad[pl.ds(0, F_IN), :] = w_raw[...]

    ag = [dict() for _ in range(C)]
    st = [dict() for _ in range(C)]

    def cols(h):
        return pl.ds(h * W, W)

    def project(h):
        out = mm((f_hi[...], f_lo[...]), split(w_pad[:, cols(h)]))
        G[h][x, y, p, 0] = out[:BLOCK]
        G[h][x, y, p, 1] = out[BLOCK:]

    def A1(h):
        own0, own1 = G[h].at[x, y, p, 0], G[h].at[x, y, p, 1]
        ag[h]["1"] = [send(own0, own0, XR), send(own0, own0, XL), send(own1, own1, YR), send(own1, own1, YL)]

    def A2(h):
        out = []
        for copy, ref, device in zip(
            ag[h]["1"],
            (G[h].at[xl, y, p, 0, LO], G[h].at[xr, y, p, 0, HI], G[h].at[x, yl, p, 1, LO], G[h].at[x, yr, p, 1, HI]),
            (XR, XL, YR, YL),
        ):
            copy.wait_recv()
            out.append(send(ref, ref, device))
        ag[h]["2"] = out

    def A3(h):
        arrive(ag[h]["2"])
        line0, line1 = G[h].at[:, y, p, 0], G[h].at[x, :, p, 1]
        ag[h]["3"] = [send(line0, line0, YR), send(line1, line1, XR), send(line0, line0, YL), send(line1, line1, XL)]
        ag[h]["5"] = [send(line0, line0, SIB), send(line1, line1, SIB)]

    def A4(h):
        out = []
        for copy, ref, device in zip(
            ag[h]["3"],
            (G[h].at[:, yl, p, 0, LO], G[h].at[xl, :, p, 1, LO], G[h].at[:, yr, p, 0, HI], G[h].at[xr, :, p, 1, HI]),
            (YR, XR, YL, XL),
        ):
            copy.wait_recv()
            out.append(send(ref, ref, device))
        ag[h]["4"] = out
        for line in (G[h].at[:, yl, p, 0], G[h].at[xl, :, p, 1], G[h].at[:, yr, p, 0], G[h].at[xr, :, p, 1]):
            ag[h]["5"].append(send(line, line, SIB))

    def A5(h):
        arrive(ag[h]["4"])
        for line in (G[h].at[:, yo, p, 0], G[h].at[xo, :, p, 1]):
            ag[h]["5"].append(send(line, line, SIB))

    def chain(base):
        def step(k, carry):
            slots[k] = slots[k] + slots[plan[base + k]]
            return carry
        lax.fori_loop(0, SLOTS, step, 0)

    def products(left_ref, load):
        def step(i, carry):
            out = []
            for j in range(4):
                k = i * 4 + j
                out.append(mm(split(left_ref[k]), split(load(k))))
            for j in range(4):
                slots[i * 4 + j] = out[j]
            return carry
        lax.fori_loop(0, SLOTS // 4, step, 0)

    def link_slots():
        lane = lax.broadcasted_iota(jnp.int32, (1, 128), 1)
        live = live_ref[0]
        for index, targets, prev, last in ((row_ref, ROWS, ROW_PREV, ROW_LAST), (col_ref, COLS, COL_PREV, COL_LAST)):
            held = jnp.full((1, 128), -1, jnp.int32)
            for k in range(SLOTS):
                held = jnp.where(lane == k, index[k], held)
            held = jnp.where(lane < live, held, -1)

            def find(match):
                best = jnp.max(jnp.where(match, lane, -1))
                return jnp.where(best < 0, SLOTS, best)

            def before(i, carry):
                for j in range(8):
                    k = i * 8 + j
                    plan[prev + k] = find((held == index[k]) & (lane < k))
                return carry
            lax.fori_loop(0, SLOTS // 8, before, 0)

            def final(i, carry):
                for j in range(8):
                    k = i * 8 + j
                    plan[last + k] = find(held == k)
                return carry
            lax.fori_loop(0, targets // 8, final, 0)

    def prepare():
        slots[SLOTS] = jnp.zeros(slots.shape[1:], F32)
        link_slots()
        load_tiles.wait()

        def turn(k, carry):
            tiles_t[k] = tiles[k].T
            return carry
        lax.fori_loop(0, SLOTS, turn, 0)
        ft_hi[...], ft_lo[...] = split(ft_pad[...])
        load_cot.wait()

    def F(h):
        arrive(ag[h]["5"])

        def load(k):
            c = col_ref[k]
            return G[h][c // 16, (c // 4) % 4, (c // 2) % 2, c % 2]
        products(tiles, load)
        chain(ROW_PREV)
        for i in range(2 * SIDE):
            part[h][i // 2, i % 2] = slots[plan[ROW_LAST + i]]

    def Z1(h):
        st[h]["z"] = [send(part[h].at[at(z, d)], zfin[h].at[d - 1], dev(dz=d)) for d in (1, 3, 2)]

    def Z3(h):
        arrive(st[h]["z"])
        for b in range(2):
            rows = pl.ds(b * BLOCK, BLOCK)
            s = (part[h][z, b] + zfin[h][0, b]) + (zfin[h][1, b] + zfin[h][2, b])
            sigma = jax.nn.sigmoid(s)
            act_ref[rows, cols(h)] = s * sigma
            GG[h][z, b] = cot[rows, cols(h)] * sigma * (1.0 + s * (1.0 - sigma))
        own = GG[h].at[z]
        st[h]["g"] = [send(own, own, dev(dz=d)) for d in (1, 3, 2)]

    def B(h):
        arrive(st[h]["g"])

        def load(k):
            c = row_ref[k]
            return GG[h][c // 2, c % 2]
        products(tiles_t, load)
        chain(COL_PREV)
        for copies in ag[h].values():
            left(copies)

        def place(core):
            def step(i, carry):
                for b in range(2):
                    G[h][i // 4, i % 4, core, b] = slots[plan[COL_LAST + i * 4 + core * 2 + b]]
                return carry
            lax.fori_loop(0, 16, step, 0)
        place(q)
        st[h]["sib"] = [send(G[h].at[:, :, q], R0[h], SIB)]
        place(p)

    def R1(h):
        arrive(st[h]["sib"])
        s, m, f = R0[h], m1[h], f1[h]

        def add(i, carry):
            s[i // 4, i % 4] = s[i // 4, i % 4] + G[h][i // 4, i % 4, p]
            return carry
        lax.fori_loop(0, 16, add, 0)
        st[h]["m1"] = [
            send(s.at[xo, :, 0, LO], m.at[0, 0], XR), send(s.at[:, yo, 1, LO], m.at[1, 0], YR),
            send(s.at[xo, :, 0, HI], m.at[0, 1], XL), send(s.at[:, yo, 1, HI], m.at[1, 1], YL)]
        st[h]["f1"] = [
            send(s.at[xr, :, 0, HI], f.at[0, 0, :, HI], XR), send(s.at[:, yr, 1, HI], f.at[1, 0, :, HI], YR),
            send(s.at[xl, :, 0, LO], f.at[0, 1, :, LO], XL), send(s.at[:, yl, 1, LO], f.at[1, 1, :, LO], YL)]

    def R2(h):
        s, m, f = R0[h], m1[h], f1[h]
        mid = st[h]["m1"]
        out = st[h]["f1"]
        mid[0].wait_recv()
        s[xr, :, 0, LO] = s[xr, :, 0, LO] + m[0, 0]
        out.append(send(s.at[xr, :, 0, LO], f.at[0, 0, :, LO], XR))
        mid[1].wait_recv()
        s[:, yr, 1, LO] = s[:, yr, 1, LO] + m[1, 0]
        out.append(send(s.at[:, yr, 1, LO], f.at[1, 0, :, LO], YR))
        mid[2].wait_recv()
        s[xl, :, 0, HI] = s[xl, :, 0, HI] + m[0, 1]
        out.append(send(s.at[xl, :, 0, HI], f.at[0, 1, :, HI], XL))
        mid[3].wait_recv()
        s[:, yl, 1, HI] = s[:, yl, 1, HI] + m[1, 1]
        out.append(send(s.at[:, yl, 1, HI], f.at[1, 1, :, HI], YL))

    def R3(h):
        arrive(st[h]["f1"])
        s, f = R0[h], f1[h]
        f[0, 0] = f[0, 0] + f[0, 1] + s[x, :, 0]
        f[1, 0] = f[1, 0] + f[1, 1] + s[:, y, 1]
        t0, t1, m, g = f.at[0, 0], f.at[1, 0], m2[h], f2[h]
        st[h]["m2"] = [
            send(t0.at[yo, LO], m.at[0, 0], YR), send(t1.at[xo, LO], m.at[1, 0], XR),
            send(t0.at[yo, HI], m.at[0, 1], YL), send(t1.at[xo, HI], m.at[1, 1], XL)]
        st[h]["f2"] = [
            send(t0.at[yr, HI], g.at[0, 0, HI], YR), send(t1.at[xr, HI], g.at[1, 0, HI], XR),
            send(t0.at[yl, LO], g.at[0, 1, LO], YL), send(t1.at[xl, LO], g.at[1, 1, LO], XL)]

    def R4(h):
        t, m, g = f1[h], m2[h], f2[h]
        mid = st[h]["m2"]
        out = st[h]["f2"]
        for copy, (b, i), rows, target, device in zip(
            mid, ((0, 0), (1, 0), (0, 1), (1, 1)), (LO, LO, HI, HI), (yr, xr, yl, xl), (YR, XR, YL, XL)
        ):
            copy.wait_recv()
            t[b, 0, target, rows] = t[b, 0, target, rows] + m[b, i]
            out.append(send(t.at[b, 0, target, rows], g.at[b, i, rows], device))

    def R5(h):
        arrive(st[h]["f2"])
        t, g = f1[h], f2[h]
        prop[pl.ds(0, BLOCK), cols(h)] = t[0, 0, y] + g[0, 0] + g[0, 1]
        prop[pl.ds(BLOCK, BLOCK), cols(h)] = t[1, 0, x] + g[1, 0] + g[1, 1]
        out = mm((ft_hi[...], ft_lo[...]), split(prop[:, cols(h)]))
        gwl[h][...] = out.reshape(2, SIDE, PAD // 8, W)
        st[h]["w1"] = [send(gwl[h].at[q], sb[h], SIB)]

    summed = []

    def grad_features(h):
        out = mm_nt(split(w_pad[:, cols(h)]), split(prop[:, cols(h)]))
        summed.append(h)
        if len(summed) == 1:
            gf_acc[...] = out
        else:
            gf_acc[...] = gf_acc[...] + out
        if len(summed) == C:
            gf_ref[...] = gf_acc[pl.ds(0, F_IN), :]

    def W2(h):
        arrive(st[h]["w1"])
        sb[h][...] = sb[h][...] + gwl[h][p]
        zb[h][z] = sb[h][z]
        st[h]["w2"] = [send(sb[h].at[at(z, d)], zb[h].at[z], dev(dz=d)) for d in (1, 2, 3)]

    def W3(h):
        arrive(st[h]["w2"])
        b = zb[h]
        xb[h][x] = (b[0] + b[1]) + (b[2] + b[3])
        own = xb[h].at[x]
        st[h]["w3"] = [send(own, own, dev(dx=d)) for d in (1, 2, 3)]

    def W4(h):
        arrive(st[h]["w3"])
        b = xb[h]
        yb[h][y] = (b[0] + b[1]) + (b[2] + b[3])
        own = yb[h].at[y]
        st[h]["w4"] = [send(own, own, dev(dy=d)) for d in (1, 2, 3)]

    def W5(h):
        arrive(st[h]["w4"])
        b = yb[h]
        gwo[h][p, z] = (b[0] + b[1]) + (b[2] + b[3])
        own = gwo[h].at[p, z]
        st[h]["w5"] = [send(own, own, dev(dz=d)) for d in (1, 2, 3)]

    def W6(h):
        arrive(st[h]["w5"])
        own = gwo[h].at[p]
        st[h]["w6"] = [send(own, own, SIB)]

    def W7(h):
        arrive(st[h]["w6"])
        gw_ref[:, cols(h)] = gwo[h][...].reshape(PAD, W)[:F_IN]

    stages = dict(P=project, A1=A1, A2=A2, A3=A3, A4=A4, A5=A5, F=F, Z1=Z1, Z3=Z3, B=B,
                  R1=R1, R2=R2, R3=R3, R4=R4, R5=R5, GF=grad_features, W2=W2, W3=W3, W4=W4, W5=W5, W6=W6, W7=W7)

    project(0)
    pl.semaphore_wait(barrier, len(peers))
    for name in " ".join(ORDER).split()[1:]:
        if name == "prep":
            prepare()
        else:
            stage, h = name.split("_")
            stages[stage](int(h))
    for copy in list(sent):
        copy.wait_send()


ORDER = (
    "P_0 A1_0 P_1 A1_1",
    "A2_0 P_2 A1_2 A2_1",
    "P_3 A3_0 A2_2 A1_3",
    "A4_0 A3_1 prep A5_0",
    "A3_2 F_0 Z1_0 A4_1",
    "A4_2 Z3_0 A2_3 A5_1",
    "F_1 Z1_1 A5_2 A3_3",
    "F_2 Z1_2 B_0 A4_3",
    "Z3_1 R1_0 A5_3 Z3_2",
    "F_3 R2_0 Z1_3 B_1",
    "R3_0 B_2 R4_0 R1_1",
    "Z3_3 R2_1 R1_2 B_3",
    "R3_1 R2_2 R5_0 R4_1",
    "R1_3 R2_3 W2_0 R5_1",
    "W2_1 R3_2 R3_3 R4_2",
    "R4_3 W3_1 R5_2 W3_0",
    "R5_3 W2_2 W2_3 W4_1",
    "GF_3 W3_2 GF_1 W4_0",
    "W5_1 W3_3 W4_2 W4_3",
    "W6_1 W5_0 W5_2 W5_3",
    "GF_2 W6_2 W6_0 W7_1",
    "W6_3 W7_2 W7_0 GF_0",
    "W7_3",
)


def body(features, weight, cotangent, tile_values, tile_row, tile_col, tile_count):
    hidden = weight.shape[1]
    nodes, width = features.shape
    C = CHUNKS
    W = hidden // C

    def vmem(*shape, dtype=F32, count=C):
        return [pltpu.VMEM(shape, dtype)] * count

    scratch = (
        vmem(4, 4, 2, 2, BLOCK, W)
        + vmem(4, 4, 2, BLOCK, W)
        + vmem(4, 2, BLOCK, W)
        + vmem(3, 2, BLOCK, W)
        + vmem(4, 2, BLOCK, W)
        + vmem(2, 2, 4, HALF, W)
        + vmem(2, 2, 4, BLOCK, W)
        + vmem(2, 2, HALF, W)
        + vmem(2, 2, BLOCK, W)
        + vmem(2, 4, PAD // 8, W)
        + vmem(4, PAD // 8, W)
        + vmem(4, PAD // 8, W)
        + vmem(4, PAD // 8, W)
        + vmem(4, PAD // 8, W)
        + vmem(2, 4, PAD // 8, W)
        + [
            pltpu.VMEM((SLOTS + 1, BLOCK, W), F32),
            pltpu.VMEM((SLOTS, BLOCK, BLOCK), F32),
            pltpu.VMEM((SLOTS, BLOCK, BLOCK), F32),
            pltpu.VMEM((width, hidden), F32),
            pltpu.VMEM((PAD, hidden), F32),
            pltpu.VMEM((width, nodes), F32),
            pltpu.VMEM((nodes, hidden), F32),
            pltpu.VMEM((nodes, PAD), BF16),
            pltpu.VMEM((nodes, PAD), BF16),
            pltpu.VMEM((PAD, nodes), BF16),
            pltpu.VMEM((PAD, nodes), BF16),
            pltpu.VMEM((nodes, hidden), F32),
            pltpu.VMEM((PAD, nodes), F32),
            pltpu.SMEM((2 * SLOTS + ROWS + COLS,), jnp.int32),
            pltpu.SemaphoreType.DMA((COPIES,)),
            pltpu.SemaphoreType.DMA((COPIES,)),
            pltpu.SemaphoreType.DMA((4,)),
        ]
    )
    whole = pl.BlockSpec(memory_space=pltpu.VMEM)
    scalars = pl.BlockSpec(memory_space=pltpu.SMEM)
    hbm = pl.BlockSpec(memory_space=pl.ANY)
    activated, grad_features, grad_weight = pl.pallas_call(
        kernel,
        out_shape=(
            jax.ShapeDtypeStruct((nodes, hidden), F32),
            jax.ShapeDtypeStruct((width, nodes), F32),
            jax.ShapeDtypeStruct((width, hidden), F32),
        ),
        in_specs=[scalars] * 3 + [hbm] * 4,
        out_specs=(whole, whole, whole),
        scratch_shapes=scratch,
        compiler_params=pltpu.CompilerParams(
            collective_id=0, has_side_effects=True, vmem_limit_bytes=62 * 1024 * 1024),
    )(tile_row, tile_col, tile_count, features.T, weight, cotangent, tile_values)
    return activated, grad_features.T, grad_weight


def solution(mesh):
    in_specs = (
        P(("rows", "rep"), None),
        P(),
        P(("rows", "rep"), None),
        P(("rows", "rep"), None, None),
        P(("rows", "rep")),
        P(("rows", "rep")),
        P(("rows", "rep")),
    )
    out_specs = (P(("rows", "rep"), None), P(("rows", "rep"), None), P())
    return jax.shard_map(body, mesh=mesh, in_specs=in_specs, out_specs=out_specs, check_vma=False)
```

```python
import functools
import math

import jax
import jax.numpy as jnp
from jax import lax
from jax.experimental import pallas as pl
from jax.experimental.pallas import tpu as pltpu
from jax.sharding import PartitionSpec as P

MESH = pl.DeviceIdType.MESH
F32 = jnp.float32
BF16 = jnp.bfloat16

BLOCK = 128
HALF = BLOCK // 2
SLOTS = 32
CHUNKS = 4
SIDE = 4
PAD = 640
GROUPS = 19

ROWS, COLS = 8, 64
ROW_PREV, ROW_LAST, COL_PREV, COL_LAST = 0, SLOTS, SLOTS + ROWS, 2 * SLOTS + ROWS

LO, HI = pl.ds(0, HALF), pl.ds(HALF, HALF)
GATHER = ("a1", "a2", "a3", "a4", "a5")


def split(value):
    high = value.astype(BF16)
    return high, (value - high.astype(F32)).astype(BF16)


def mm(a, b):
    left = jnp.concatenate([a[0], a[1], a[0]], axis=1)
    right = jnp.concatenate([b[0], b[0], b[1]], axis=0)
    return jnp.dot(left, right, preferred_element_type=F32)


def mm_nt(a, b):
    left = jnp.concatenate([a[0], a[1], a[0]], axis=1)
    right = jnp.concatenate([b[0], b[0], b[1]], axis=1)
    return lax.dot_general(left, right, (((1,), (1,)), ((), ())), preferred_element_type=F32)


def kernel(*refs):
    C = CHUNKS
    row_ref, col_ref, live_ref, f_hbm, w_hbm, cot_hbm, tiles_hbm, act_hbm, gf_hbm, gw_hbm = refs[:10]
    refs = list(refs[10:])

    def take(count):
        out = refs[:count]
        del refs[:count]
        return out

    G, R0, part, zmid, zfin, GG = (take(C) for _ in range(6))
    m1, f1, m2, f2 = (take(C) for _ in range(4))
    gwl, sb, wa, wb, wc, gwo = (take(C) for _ in range(6))
    slots, tiles, tiles_t, w_raw, w_pad, f_raw, cot, f_hi, f_lo, ft_hi, ft_lo, prop, gf_acc, plan = take(14)
    act, gf, gw = take(3)
    send_sem, recv_sem, load_sem, store_sem = take(4)
    W = prop.shape[1] // C

    r = lax.axis_index("rows")
    z = lax.axis_index("rep")
    x, y, p = r // 8, (r // 2) % 4, r % 2
    q = 1 - p

    def at(i, d):
        return (i + d) % SIDE

    def dev(dx=0, dy=0, dz=0, core=None):
        c = p if core is None else core
        return (at(x, dx) * 8 + at(y, dy) * 2 + c, at(z, dz))

    xl, xr, xo = at(x, 3), at(x, 1), at(x, 2)
    yl, yr, yo = at(y, 3), at(y, 1), at(y, 2)
    zl, zr, zo = at(z, 3), at(z, 1), at(z, 2)
    XR, XL, YR, YL, ZR, ZL = dev(dx=1), dev(dx=3), dev(dy=1), dev(dy=3), dev(dz=1), dev(dz=3)
    SIB = dev(core=q)

    stores = []

    def store(src, dst):
        copy = pltpu.make_async_copy(src, dst, store_sem.at[len(stores)])
        copy.start()
        stores.append(copy)

    ready = []

    def need(load):
        if not any(load is other for other in ready):
            load.wait()
            ready.append(load)

    names = [[] for _ in range(C)]
    lines = {}
    leaving = []

    def spot(group):
        chunk, name = group
        if name not in names[chunk]:
            names[chunk].append(name)
        return GROUPS * chunk + names[chunk].index(name)

    def send(src, dst, device, group):
        copy = pltpu.make_async_remote_copy(
            src_ref=src, dst_ref=dst, send_sem=send_sem.at[spot(group)], recv_sem=recv_sem.at[spot(group)],
            device_id=device, device_id_type=MESH)
        copy.start()
        if group not in lines:
            lines[group] = 0
            leaving.append(group)
        lines[group] += math.prod(src.shape) // W

    def all_of(group):
        count = lines[group]
        ref = slots.at[pl.ds(0, count // BLOCK)] if count % BLOCK == 0 else sb[0].at[pl.ds(0, count)]
        return pltpu.make_async_remote_copy(
            src_ref=ref, dst_ref=ref, send_sem=send_sem.at[spot(group)], recv_sem=recv_sem.at[spot(group)],
            device_id=XR, device_id_type=MESH)

    def arrive(*group):
        all_of(group).wait_recv()

    def left(h, *which):
        for name in which:
            all_of((h, name)).wait_send()
            leaving.remove((h, name))

    def drain():
        for group in list(leaving):
            left(*group)

    loads = [
        pltpu.make_async_copy(src, dst, load_sem.at[i])
        for i, (src, dst) in enumerate(((f_hbm, f_raw), (w_hbm, w_raw), (cot_hbm, cot), (tiles_hbm, tiles)))
    ]
    load_f, load_w, load_cot, load_tiles = loads
    load_f.start()
    load_w.start()

    barrier = pltpu.get_barrier_semaphore()
    peers = [dev(dx=d) for d in (1, 2, 3)] + [dev(dy=d) for d in (1, 2, 3)] + [dev(dz=d) for d in (1, 2, 3)] + [SIB]
    for peer in peers:
        pl.semaphore_signal(barrier, inc=1, device_id=peer, device_id_type=MESH)

    F_IN = f_hbm.shape[0]
    tail = F_IN // 8 * 8
    ft_pad = gf_acc
    load_f.wait()
    ft_pad[pl.ds(tail, PAD - tail), :] = jnp.zeros((PAD - tail, ft_pad.shape[1]), F32)
    ft_pad[pl.ds(0, F_IN), :] = f_raw[...]
    f_hi[...], f_lo[...] = split(ft_pad[...].T)
    load_w.wait()
    w_pad[pl.ds(tail, PAD - tail), :] = jnp.zeros((PAD - tail, w_pad.shape[1]), F32)
    w_pad[pl.ds(0, F_IN), :] = w_raw[...]

    def cols(h):
        return pl.ds(h * W, W)

    def project(h):
        out = mm((f_hi[...], f_lo[...]), split(w_pad[:, cols(h)]))
        G[h][x, y, p, 0] = out[:BLOCK]
        G[h][x, y, p, 1] = out[BLOCK:]

    def A1(h):
        own0, own1 = G[h].at[x, y, p, 0], G[h].at[x, y, p, 1]
        g = (h, "a1")
        for ref, device in ((own0, XR), (own0, XL), (own1, YR), (own1, YL)):
            send(ref, ref, device, g)

    def A2(h):
        arrive(h, "a1")
        for ref, device in (
            (G[h].at[xl, y, p, 0, LO], XR), (G[h].at[xr, y, p, 0, HI], XL),
            (G[h].at[x, yl, p, 1, LO], YR), (G[h].at[x, yr, p, 1, HI], YL),
        ):
            send(ref, ref, device, (h, "a2"))

    def A3(h):
        arrive(h, "a2")
        line0, line1 = G[h].at[:, y, p, 0], G[h].at[x, :, p, 1]
        for line, device in ((line0, YR), (line1, XR), (line0, YL), (line1, XL)):
            send(line, line, device, (h, "a3"))
        for line in (line0, line1):
            send(line, line, SIB, (h, "a5"))

    def A4(h):
        arrive(h, "a3")
        for ref, device in (
            (G[h].at[:, yl, p, 0, LO], YR), (G[h].at[xl, :, p, 1, LO], XR),
            (G[h].at[:, yr, p, 0, HI], YL), (G[h].at[xr, :, p, 1, HI], XL),
        ):
            send(ref, ref, device, (h, "a4"))
        for line in (G[h].at[:, yl, p, 0], G[h].at[xl, :, p, 1], G[h].at[:, yr, p, 0], G[h].at[xr, :, p, 1]):
            send(line, line, SIB, (h, "a5"))

    def A5(h):
        arrive(h, "a4")
        for line in (G[h].at[:, yo, p, 0], G[h].at[xo, :, p, 1]):
            send(line, line, SIB, (h, "a5"))

    def chain(base):
        def step(k, carry):
            slots[k] = slots[k] + slots[plan[base + k]]
            return carry
        lax.fori_loop(0, SLOTS, step, 0)

    def products(left_ref, load):
        def step(i, carry):
            out = []
            for j in range(4):
                k = i * 4 + j
                out.append(mm(split(left_ref[k]), split(load(k))))
            for j in range(4):
                slots[i * 4 + j] = out[j]
            return carry
        lax.fori_loop(0, SLOTS // 4, step, 0)

    def link_slots():
        lane = lax.broadcasted_iota(jnp.int32, (1, 128), 1)
        live = live_ref[0]
        for index, targets, prev, last in ((row_ref, ROWS, ROW_PREV, ROW_LAST), (col_ref, COLS, COL_PREV, COL_LAST)):
            held = jnp.full((1, 128), -1, jnp.int32)
            for k in range(SLOTS):
                held = jnp.where(lane == k, index[k], held)
            held = jnp.where(lane < live, held, -1)

            def find(match):
                best = jnp.max(jnp.where(match, lane, -1))
                return jnp.where(best < 0, SLOTS, best)

            def before(i, carry):
                for j in range(8):
                    k = i * 8 + j
                    plan[prev + k] = find((held == index[k]) & (lane < k))
                return carry
            lax.fori_loop(0, SLOTS // 8, before, 0)

            def final(i, carry):
                for j in range(8):
                    k = i * 8 + j
                    plan[last + k] = find(held == k)
                return carry
            lax.fori_loop(0, targets // 8, final, 0)

    def link():
        slots[SLOTS] = jnp.zeros(slots.shape[1:], F32)
        link_slots()

    def turn_tiles():
        def turn(k, carry):
            tiles_t[k] = tiles[k].T
            return carry
        need(load_tiles)
        lax.fori_loop(0, SLOTS, turn, 0)

    def split_features():
        ft_hi[...], ft_lo[...] = split(ft_pad[...])

    def F(h):
        need(load_tiles)
        arrive(h, "a5")

        def load(k):
            c = col_ref[k]
            return G[h][c // 16, (c // 4) % 4, (c // 2) % 2, c % 2]
        products(tiles, load)
        chain(ROW_PREV)
        for i in range(2 * SIDE):
            part[h][i // 2, i % 2] = slots[plan[ROW_LAST + i]]

    def Z1(h):
        a, b = part[h], zfin[h]
        send(a.at[zo, 0], zmid[h].at[0], ZR, (h, "z1"))
        send(a.at[zo, 1], zmid[h].at[1], ZL, (h, "z1"))
        send(a.at[zr, 1], b.at[0, 1], ZR, (h, "z2"))
        send(a.at[zl, 0], b.at[1, 0], ZL, (h, "z2"))

    def Z2(h):
        a, b = part[h], zfin[h]
        arrive(h, "z1")
        a[zr, 0] = a[zr, 0] + zmid[h][0]
        send(a.at[zr, 0], b.at[0, 0], ZR, (h, "z2"))
        a[zl, 1] = a[zl, 1] + zmid[h][1]
        send(a.at[zl, 1], b.at[1, 1], ZL, (h, "z2"))

    def Z3(h):
        arrive(h, "z2")
        need(load_cot)
        for b in range(2):
            rows = pl.ds(b * BLOCK, BLOCK)
            s = part[h][z, b] + zfin[h][0, b] + zfin[h][1, b]
            sigma = jax.nn.sigmoid(s)
            act[rows, cols(h)] = s * sigma
            GG[h][z, b] = cot[rows, cols(h)] * sigma * (1.0 + s * (1.0 - sigma))
        store(act.at[:, cols(h)], act_hbm.at[:, cols(h)])
        own = GG[h].at[z]
        for d in (1, 3, 2):
            send(own, own, dev(dz=d), (h, "g"))

    def B(h):
        arrive(h, "g")

        def load(k):
            c = row_ref[k]
            return GG[h][c // 2, c % 2]
        products(tiles_t, load)
        chain(COL_PREV)
        left(h, *GATHER)

        def place(core, b):
            def step(i, carry):
                for j in range(2):
                    k = i * 2 + j
                    G[h][k // 4, k % 4, core, b] = slots[plan[COL_LAST + k * 4 + core * 2 + b]]
                return carry
            lax.fori_loop(0, 8, step, 0)
        for b in range(2):
            place(q, b)
            send(G[h].at[:, :, q, b], R0[h].at[:, :, b], SIB, (h, "s" + str(b)))
        for b in range(2):
            place(p, b)

    def with_own(h, b):
        arrive(h, "s" + str(b))
        s = R0[h]

        def add(i, carry):
            s[i // 4, i % 4, b] = s[i // 4, i % 4, b] + G[h][i // 4, i % 4, p, b]
            return carry
        lax.fori_loop(0, 16, add, 0)

    def R1a(h):
        with_own(h, 0)
        s, m, f = R0[h], m1[h], f1[h]
        send(s.at[xo, :, 0, LO], m.at[0, 0], XR, (h, "m1"))
        send(s.at[xo, :, 0, HI], m.at[0, 1], XL, (h, "m1"))
        send(s.at[xr, :, 0, HI], f.at[0, 0, :, HI], XR, (h, "f1"))
        send(s.at[xl, :, 0, LO], f.at[0, 1, :, LO], XL, (h, "f1"))

    def R1b(h):
        with_own(h, 1)
        s, m, f = R0[h], m1[h], f1[h]
        send(s.at[:, yo, 1, LO], m.at[1, 0], YR, (h, "m1"))
        send(s.at[:, yo, 1, HI], m.at[1, 1], YL, (h, "m1"))
        send(s.at[:, yr, 1, HI], f.at[1, 0, :, HI], YR, (h, "f1"))
        send(s.at[:, yl, 1, LO], f.at[1, 1, :, LO], YL, (h, "f1"))

    def R2(h):
        s, m, f = R0[h], m1[h], f1[h]
        g = (h, "f1")
        arrive(h, "m1")
        s[xr, :, 0, LO] = s[xr, :, 0, LO] + m[0, 0]
        send(s.at[xr, :, 0, LO], f.at[0, 0, :, LO], XR, g)
        s[:, yr, 1, LO] = s[:, yr, 1, LO] + m[1, 0]
        send(s.at[:, yr, 1, LO], f.at[1, 0, :, LO], YR, g)
        s[xl, :, 0, HI] = s[xl, :, 0, HI] + m[0, 1]
        send(s.at[xl, :, 0, HI], f.at[0, 1, :, HI], XL, g)
        s[:, yl, 1, HI] = s[:, yl, 1, HI] + m[1, 1]
        send(s.at[:, yl, 1, HI], f.at[1, 1, :, HI], YL, g)

    def R3(h):
        arrive(h, "f1")
        s, f = R0[h], f1[h]
        f[0, 0] = f[0, 0] + f[0, 1] + s[x, :, 0]
        f[1, 0] = f[1, 0] + f[1, 1] + s[:, y, 1]
        t0, t1, m, b = f.at[0, 0], f.at[1, 0], m2[h], f2[h]
        g = (h, "f2")
        if h == C - 1:
            send(t0.at[yr], b.at[0, 0], YR, g)
            send(t1.at[xr], b.at[1, 0], XR, g)
            send(t0.at[yl], b.at[0, 1], YL, g)
            send(t1.at[xl], b.at[1, 1], XL, g)
            send(t0.at[yo], m.at[0], dev(dy=2), g)
            send(t1.at[xo], m.at[1], dev(dx=2), g)
            return
        send(t0.at[yo, LO], m.at[0, 0], YR, (h, "m2"))
        send(t1.at[xo, LO], m.at[1, 0], XR, (h, "m2"))
        send(t0.at[yo, HI], m.at[0, 1], YL, (h, "m2"))
        send(t1.at[xo, HI], m.at[1, 1], XL, (h, "m2"))
        send(t0.at[yr, HI], b.at[0, 0, HI], YR, g)
        send(t1.at[xr, HI], b.at[1, 0, HI], XR, g)
        send(t0.at[yl, LO], b.at[0, 1, LO], YL, g)
        send(t1.at[xl, LO], b.at[1, 1, LO], XL, g)

    def R4(h):
        if h == C - 1:
            return
        t, m, b = f1[h], m2[h], f2[h]
        arrive(h, "m2")
        for (i, j), rows, target, device in zip(
            ((0, 0), (1, 0), (0, 1), (1, 1)), (LO, LO, HI, HI), (yr, xr, yl, xl), (YR, XR, YL, XL)
        ):
            t[i, 0, target, rows] = t[i, 0, target, rows] + m[i, j]
            send(t.at[i, 0, target, rows], b.at[i, j, rows], device, (h, "f2"))

    def R5(h):
        arrive(h, "f2")
        t, g = f1[h], f2[h]
        own0, own1 = t[0, 0, y] + g[0, 0] + g[0, 1], t[1, 0, x] + g[1, 0] + g[1, 1]
        if h == C - 1:
            own0, own1 = own0 + m2[h][0], own1 + m2[h][1]
        prop[pl.ds(0, BLOCK), cols(h)] = own0
        prop[pl.ds(BLOCK, BLOCK), cols(h)] = own1
        right = split(prop[:, cols(h)])

        def weight_half(core):
            rows = pl.ds(pl.multiple_of(core * (PAD // 2), PAD // 2), PAD // 2)
            gwl[h][core] = mm((ft_hi[rows, :], ft_lo[rows, :]), right)
        weight_half(q)
        send(gwl[h].at[q], sb[h], SIB, (h, "w1"))
        weight_half(p)

    summed = []

    def grad_features(h):
        out = mm_nt(split(w_pad[:, cols(h)]), split(prop[:, cols(h)]))
        summed.append(h)
        if len(summed) == 1:
            gf_acc[...] = out
        else:
            gf_acc[...] = gf_acc[...] + out
        if len(summed) == C:
            gf[...] = gf_acc[pl.ds(0, F_IN), :]
            store(gf, gf_hbm)

    me = dict(x=x, y=y, z=z)

    def peers_of(axis):
        return [(at(me[axis], d), dev(**{"d" + axis: d})) for d in (1, 3, 2)]

    def groups(h):
        if h < C - 1:
            return [(0, PAD // 8, pl.ds(0, PAD // 8), "zxyz")]
        n = PAD // 16
        return [(0, n, pl.ds(0, n), "zxyz"), (4 * n, n, pl.ds(n, n), "yzxy")]

    def piece(first, n, i):
        return pl.ds(pl.multiple_of(first + i * n, 8), n)

    def total(b, part_of):
        return (b[0, part_of] + b[1, part_of]) + (b[2, part_of] + b[3, part_of])

    def W2(h):
        arrive(h, "w1")
        sb[h][...] = sb[h][...] + gwl[h][p]
        for first, n, spot, axes in groups(h):
            mine = me[axes[0]]
            wa[h][mine, spot] = sb[h][piece(first, n, mine)]
            for i, device in peers_of(axes[0]):
                send(sb[h].at[piece(first, n, i)], wa[h].at[mine, spot], device, (h, "w2"))

    def exchange(h, before, after, source, target, step):
        arrive(h, before)
        for first, n, spot, axes in groups(h):
            mine = me[axes[step]]
            target[mine, spot] = total(source, spot)
            own = target.at[mine, spot]
            for i, device in peers_of(axes[step]):
                send(own, own, device, (h, after))

    def W3(h):
        exchange(h, "w2", "w3", wa[h], wb[h], 1)

    def W4(h):
        exchange(h, "w3", "w4", wb[h], wc[h], 2)

    def W5(h):
        arrive(h, "w4")
        for first, n, spot, axes in groups(h):
            rows = piece(first, n, me[axes[3]])
            gwo[h][p, rows] = total(wc[h], spot)
            own = gwo[h].at[p, rows]
            for i, device in peers_of(axes[3]):
                send(own, own, device, (h, "w5"))

    def W6(h):
        arrive(h, "w5")
        own = gwo[h].at[p]
        send(own, own, SIB, (h, "w6"))

    def W7(h):
        arrive(h, "w6")
        half = PAD // 2
        gw[pl.ds(0, half), cols(h)] = gwo[h][0]
        gw[pl.ds(half, F_IN - half), cols(h)] = gwo[h][1, pl.ds(0, F_IN - half)]
        store(gw.at[:, cols(h)], gw_hbm.at[:, cols(h)])

    stages = dict(P=project, A1=A1, A2=A2, A3=A3, A4=A4, A5=A5, F=F, Z1=Z1, Z2=Z2, Z3=Z3, B=B,
                  R1a=R1a, R1b=R1b, R2=R2, R3=R3, R4=R4, R5=R5, GF=grad_features, W2=W2, W3=W3, W4=W4, W5=W5, W6=W6, W7=W7)

    alone = dict(plan=link, turn=turn_tiles, ft=split_features, drain=drain)
    project(0)
    load_tiles.start()
    load_cot.start()
    pl.semaphore_wait(barrier, len(peers))
    for name in " ".join(ORDER).split()[1:]:
        if name in alone:
            alone[name]()
        else:
            stage, h = name.split("_")
            stages[stage](int(h))
    drain()
    for copy in stores:
        copy.wait()


ORDER = (
    "P_0 P_1 A1_1 P_2",
    "P_3 A1_0 A2_1 A1_2",
    "A1_3 ft A3_1 A2_0",
    "turn A2_2 plan A2_3",
    "A4_1 A3_0 A3_2 A5_1",
    "F_1 Z1_1 Z2_1 A4_0",
    "A4_2 A3_3 Z3_1 A5_0",
    "A5_2 F_0 Z1_0 F_2",
    "Z1_2 B_1 Z2_0 A4_3",
    "Z2_2 R1a_1 Z3_0 R1b_1",
    "Z3_2 A5_3 F_3 Z1_3",
    "R2_1 B_0 R3_1 R1a_0",
    "Z2_3 R4_1 R1b_0 B_2",
    "Z3_3 R2_0 R1b_2 R1a_2",
    "R5_1 GF_1 R3_0 B_3",
    "R2_2 R4_0 R1a_3 W2_1",
    "R1b_3 R5_0 R3_2 GF_0",
    "R2_3 W2_0 R4_2 W3_1",
    "R3_3 R5_2 W4_1 GF_2",
    "W2_2 W3_0 R4_3 R5_3",
    "GF_3 W3_2 W2_3 W4_0",
    "W5_1 W3_3 W4_2 W6_1",
    "W5_0 drain W4_3 W5_2",
    "W6_0 W5_3 W7_0 W6_2",
    "W7_1 W6_3 W7_2 W7_3",
)


def hand_over(*refs):
    copies = [pltpu.make_async_copy(refs[i], refs[3 + i], refs[6].at[i]) for i in range(3)]
    for copy in copies:
        copy.start()
    for copy in copies:
        copy.wait()


def body(features, weight, cotangent, tile_values, tile_row, tile_col, tile_count):
    hidden = weight.shape[1]
    nodes, width = features.shape
    C = CHUNKS
    W = hidden // C

    def vmem(*shape, dtype=F32, count=C):
        return [pltpu.VMEM(shape, dtype)] * count

    scratch = (
        vmem(4, 4, 2, 2, BLOCK, W)
        + vmem(4, 4, 2, BLOCK, W)
        + vmem(4, 2, BLOCK, W)
        + vmem(2, BLOCK, W)
        + vmem(2, 2, BLOCK, W)
        + vmem(4, 2, BLOCK, W)
        + vmem(2, 2, 4, HALF, W)
        + vmem(2, 2, 4, BLOCK, W)
        + vmem(2, 2, HALF, W, count=C - 1)
        + vmem(2, BLOCK, W, count=1)
        + vmem(2, 2, BLOCK, W)
        + vmem(2, PAD // 2, W)
        + vmem(PAD // 2, W)
        + vmem(4, PAD // 8, W)
        + vmem(4, PAD // 8, W)
        + vmem(4, PAD // 8, W)
        + vmem(2, PAD // 2, W)
        + [
            pltpu.VMEM((SLOTS + 1, BLOCK, W), F32),
            pltpu.VMEM((SLOTS, BLOCK, BLOCK), F32),
            pltpu.VMEM((SLOTS, BLOCK, BLOCK), F32),
            pltpu.VMEM((width, hidden), F32),
            pltpu.VMEM((PAD, hidden), F32),
            pltpu.VMEM((width, nodes), F32),
            pltpu.VMEM((nodes, hidden), F32),
            pltpu.VMEM((nodes, PAD), BF16),
            pltpu.VMEM((nodes, PAD), BF16),
            pltpu.VMEM((PAD, nodes), BF16),
            pltpu.VMEM((PAD, nodes), BF16),
            pltpu.VMEM((nodes, hidden), F32),
            pltpu.VMEM((PAD, nodes), F32),
            pltpu.SMEM((2 * SLOTS + ROWS + COLS,), jnp.int32),
            pltpu.VMEM((nodes, hidden), F32),
            pltpu.VMEM((width, nodes), F32),
            pltpu.VMEM((width, hidden), F32),
            pltpu.SemaphoreType.DMA((GROUPS * C,)),
            pltpu.SemaphoreType.DMA((GROUPS * C,)),
            pltpu.SemaphoreType.DMA((4,)),
            pltpu.SemaphoreType.DMA((2 * C + 1,)),
        ]
    )
    scalars = pl.BlockSpec(memory_space=pltpu.SMEM)
    hbm = pl.BlockSpec(memory_space=pl.ANY)
    shapes = (
        jax.ShapeDtypeStruct((nodes, hidden), F32),
        jax.ShapeDtypeStruct((width, nodes), F32),
        jax.ShapeDtypeStruct((width, hidden), F32),
    )
    results = pl.pallas_call(
        kernel,
        out_shape=shapes,
        in_specs=[scalars] * 3 + [hbm] * 4,
        out_specs=(hbm, hbm, hbm),
        scratch_shapes=scratch,
        compiler_params=pltpu.CompilerParams(
            collective_id=0, has_side_effects=True, vmem_limit_bytes=62 * 1024 * 1024),
    )(tile_row, tile_col, tile_count, features.T, weight, cotangent, tile_values)
    activated, grad_features, grad_weight = pl.pallas_call(
        hand_over,
        out_shape=shapes,
        in_specs=[pl.BlockSpec(memory_space=pltpu.VMEM)] * 3,
        out_specs=(hbm,) * 3,
        scratch_shapes=[pltpu.SemaphoreType.DMA((3,))],
    )(*results)
    return activated, grad_features.T, grad_weight


def solution(mesh):
    in_specs = (
        P(("rows", "rep"), None),
        P(),
        P(("rows", "rep"), None),
        P(("rows", "rep"), None, None),
        P(("rows", "rep")),
        P(("rows", "rep")),
        P(("rows", "rep")),
    )
    out_specs = (P(("rows", "rep"), None), P(("rows", "rep"), None), P())
    return jax.shard_map(body, mesh=mesh, in_specs=in_specs, out_specs=out_specs, check_vma=False)
```

```python
import functools
import math

import jax
import jax.numpy as jnp
from jax import lax
from jax.experimental import pallas as pl
from jax.experimental.pallas import tpu as pltpu
from jax.sharding import PartitionSpec as P

MESH = pl.DeviceIdType.MESH
F32 = jnp.float32
BF16 = jnp.bfloat16

BLOCK = 128
HALF = BLOCK // 2
SLOTS = 32
CHUNKS = 4
SIDE = 4
PAD = 640
GROUPS = 21

ROWS, COLS = 8, 64
ROW_PREV, ROW_LAST, COL_PREV, COL_LAST = 0, SLOTS, SLOTS + ROWS, 2 * SLOTS + ROWS

LO, HI = pl.ds(0, HALF), pl.ds(HALF, HALF)
GATHER = ("a1", "a2", "a3", "a4", "a5")


def split(value):
    high = value.astype(BF16)
    return high, (value - high.astype(F32)).astype(BF16)


def mm(a, b):
    left = jnp.concatenate([a[0], a[1], a[0]], axis=1)
    right = jnp.concatenate([b[0], b[0], b[1]], axis=0)
    return jnp.dot(left, right, preferred_element_type=F32)


def mm_nt(a, b):
    left = jnp.concatenate([a[0], a[1], a[0]], axis=1)
    right = jnp.concatenate([b[0], b[0], b[1]], axis=1)
    return lax.dot_general(left, right, (((1,), (1,)), ((), ())), preferred_element_type=F32)


def kernel(*refs):
    C = CHUNKS
    row_ref, col_ref, live_ref, f_hbm, w_hbm, cot_hbm, tiles_hbm, act_hbm, gf_hbm, gw_hbm = refs[:10]
    refs = list(refs[10:])

    def take(count):
        out = refs[:count]
        del refs[:count]
        return out

    G, R0, part, zfin, GG = (take(C) for _ in range(5))
    m1, f1, m2, f2 = (take(C) for _ in range(4))
    gwl, sb, wa, wb, wc, gwo = (take(C) for _ in range(6))
    slots, tiles, tiles_t, w_raw, w_pad, f_raw, cot, f_hi, f_lo, ft_hi, ft_lo, prop, gf_acc, plan = take(14)
    act, gf, gw = take(3)
    send_sem, recv_sem, load_sem, store_sem = take(4)
    W = prop.shape[1] // C

    r = lax.axis_index("rows")
    z = lax.axis_index("rep")
    x, y, p = r // 8, (r // 2) % 4, r % 2
    q = 1 - p

    def at(i, d):
        return (i + d) % SIDE

    def dev(dx=0, dy=0, dz=0, core=None):
        c = p if core is None else core
        return (at(x, dx) * 8 + at(y, dy) * 2 + c, at(z, dz))

    xl, xr, xo = at(x, 3), at(x, 1), at(x, 2)
    yl, yr, yo = at(y, 3), at(y, 1), at(y, 2)
    zl, zr, zo = at(z, 3), at(z, 1), at(z, 2)
    XR, XL, YR, YL, ZR, ZL = dev(dx=1), dev(dx=3), dev(dy=1), dev(dy=3), dev(dz=1), dev(dz=3)
    SIB = dev(core=q)

    stores = []

    def store(src, dst):
        copy = pltpu.make_async_copy(src, dst, store_sem.at[len(stores)])
        copy.start()
        stores.append(copy)

    ready = []

    def need(load):
        if not any(load is other for other in ready):
            load.wait()
            ready.append(load)

    names = [[] for _ in range(C)]
    lines = {}
    leaving = []

    def spot(group):
        chunk, name = group
        if name not in names[chunk]:
            names[chunk].append(name)
        return GROUPS * chunk + names[chunk].index(name)

    def send(src, dst, device, group):
        copy = pltpu.make_async_remote_copy(
            src_ref=src, dst_ref=dst, send_sem=send_sem.at[spot(group)], recv_sem=recv_sem.at[spot(group)],
            device_id=device, device_id_type=MESH)
        copy.start()
        if group not in lines:
            lines[group] = 0
            leaving.append(group)
        lines[group] += math.prod(src.shape) // W

    def all_of(group):
        count = lines[group]
        ref = slots.at[pl.ds(0, count // BLOCK)] if count % BLOCK == 0 else sb[0].at[pl.ds(0, count)]
        return pltpu.make_async_remote_copy(
            src_ref=ref, dst_ref=ref, send_sem=send_sem.at[spot(group)], recv_sem=recv_sem.at[spot(group)],
            device_id=XR, device_id_type=MESH)

    def arrive(*group):
        all_of(group).wait_recv()

    def left(h, *which):
        for name in which:
            all_of((h, name)).wait_send()
            leaving.remove((h, name))

    def drain():
        for group in list(leaving):
            left(*group)

    loads = [
        pltpu.make_async_copy(src, dst, load_sem.at[i])
        for i, (src, dst) in enumerate(((f_hbm, f_raw), (w_hbm, w_raw), (cot_hbm, cot), (tiles_hbm, slots.at[pl.ds(0, SLOTS)])))
    ]
    load_f, load_w, load_cot, load_tiles = loads
    load_f.start()
    load_w.start()

    barrier = pltpu.get_barrier_semaphore()
    peers = [dev(dx=d) for d in (1, 2, 3)] + [dev(dy=d) for d in (1, 2, 3)] + [dev(dz=d) for d in (1, 2, 3)] + [SIB]
    for peer in peers:
        pl.semaphore_signal(barrier, inc=1, device_id=peer, device_id_type=MESH)

    F_IN = f_hbm.shape[0]
    tail = F_IN // 8 * 8
    ft_pad = gf_acc
    load_f.wait()
    ft_pad[pl.ds(tail, PAD - tail), :] = jnp.zeros((PAD - tail, ft_pad.shape[1]), F32)
    ft_pad[pl.ds(0, F_IN), :] = f_raw[...]
    f_hi[...], f_lo[...] = split(ft_pad[...].T)
    load_w.wait()
    w_pad[pl.ds(tail, PAD - tail), :] = jnp.zeros((PAD - tail, w_pad.shape[1]), F32)
    w_pad[pl.ds(0, F_IN), :] = w_raw[...]

    def cols(h):
        return pl.ds(h * W, W)

    def project(h):
        out = mm((f_hi[...], f_lo[...]), split(w_pad[:, cols(h)]))
        G[h][x, y, p, 0] = out[:BLOCK]
        G[h][x, y, p, 1] = out[BLOCK:]

    def A1(h):
        own0, own1 = G[h].at[x, y, p, 0], G[h].at[x, y, p, 1]
        g = (h, "a1")
        for ref, device in ((own0, XR), (own0, XL), (own1, YR), (own1, YL)):
            send(ref, ref, device, g)

    def A2(h):
        arrive(h, "a1")
        for ref, device in (
            (G[h].at[xl, y, p, 0, LO], XR), (G[h].at[xr, y, p, 0, HI], XL),
            (G[h].at[x, yl, p, 1, LO], YR), (G[h].at[x, yr, p, 1, HI], YL),
        ):
            send(ref, ref, device, (h, "a2"))

    def A3(h):
        arrive(h, "a2")
        line0, line1 = G[h].at[:, y, p, 0], G[h].at[x, :, p, 1]
        for line, device in ((line0, YR), (line1, XR), (line0, YL), (line1, XL)):
            send(line, line, device, (h, "a3"))
        for line in (line0, line1):
            send(line, line, SIB, (h, "a5"))

    def A4(h):
        arrive(h, "a3")
        for ref, device in (
            (G[h].at[:, yl, p, 0, LO], YR), (G[h].at[xl, :, p, 1, LO], XR),
            (G[h].at[:, yr, p, 0, HI], YL), (G[h].at[xr, :, p, 1, HI], XL),
        ):
            send(ref, ref, device, (h, "a4"))
        for line in (G[h].at[:, yl, p, 0], G[h].at[xl, :, p, 1], G[h].at[:, yr, p, 0], G[h].at[xr, :, p, 1]):
            send(line, line, SIB, (h, "a5"))

    def A5(h):
        arrive(h, "a4")
        for line in (G[h].at[:, yo, p, 0], G[h].at[xo, :, p, 1]):
            send(line, line, SIB, (h, "a5"))

    def products(left_ref, load, prev):
        def product(k):
            both = left_ref[k]
            return mm((both[:, :BLOCK], both[:, BLOCK:]), split(load(k)))

        def add(i):
            for j in range(4):
                k = i * 4 + j
                slots[k] = slots[k] + slots[plan[prev + k]]

        def put(i, out):
            for j in range(4):
                slots[i * 4 + j] = out[j]

        def step(i, carry):
            out = [product(i * 4 + j) for j in range(4)]
            add(i - 1)
            put(i, out)
            return carry
        put(0, [product(j) for j in range(4)])
        lax.fori_loop(1, SLOTS // 4, step, 0)
        add(SLOTS // 4 - 1)

    def link_slots():
        lane = lax.broadcasted_iota(jnp.int32, (1, 128), 1)
        live = live_ref[0]
        for index, targets, prev, last in ((row_ref, ROWS, ROW_PREV, ROW_LAST), (col_ref, COLS, COL_PREV, COL_LAST)):
            held = jnp.full((1, 128), -1, jnp.int32)
            for k in range(SLOTS):
                held = jnp.where(lane == k, index[k], held)
            held = jnp.where(lane < live, held, -1)

            def find(match):
                best = jnp.max(jnp.where(match, lane, -1))
                return jnp.where(best < 0, SLOTS, best)

            def before(i, carry):
                for j in range(8):
                    k = i * 8 + j
                    plan[prev + k] = find((held == index[k]) & (lane < k))
                return carry
            lax.fori_loop(0, SLOTS // 8, before, 0)

            def final(i, carry):
                for j in range(8):
                    k = i * 8 + j
                    plan[last + k] = find(held == k)
                return carry
            lax.fori_loop(0, targets // 8, final, 0)

    def link():
        slots[SLOTS] = jnp.zeros(slots.shape[1:], F32)
        link_slots()

    def turn_tiles():
        def turn(k, carry):
            tile = slots[k]
            tiles[k] = jnp.concatenate(split(tile), axis=1)
            tiles_t[k] = jnp.concatenate(split(tile.T), axis=1)
            return carry
        need(load_tiles)
        lax.fori_loop(0, SLOTS, turn, 0)

    def split_features():
        ft_hi[...], ft_lo[...] = split(ft_pad[...])

    def F(h):
        arrive(h, "a5")

        def load(k):
            c = col_ref[k]
            return G[h][c // 16, (c // 4) % 4, (c // 2) % 2, c % 2]
        products(tiles, load, ROW_PREV)
        for i in range(2 * SIDE):
            part[h][i // 2, i % 2] = slots[plan[ROW_LAST + i]]

    def Z1(h):
        for b in range(2):
            for d in (1, 3, 2):
                send(part[h].at[at(z, d), b], zfin[h].at[d - 1, b], dev(dz=d), (h, "z" + str(b)))

    def activate(h, b):
        arrive(h, "z" + str(b))
        need(load_cot)
        rows = pl.ds(b * BLOCK, BLOCK)
        s = (part[h][z, b] + zfin[h][0, b]) + (zfin[h][1, b] + zfin[h][2, b])
        sigma = jax.nn.sigmoid(s)
        act[rows, cols(h)] = s * sigma
        GG[h][z, b] = cot[rows, cols(h)] * sigma * (1.0 + s * (1.0 - sigma))
        own = GG[h].at[z, b]
        for d in (1, 3, 2):
            send(own, own, dev(dz=d), (h, "g" + str(b)))
        store(act.at[rows, cols(h)], act_hbm.at[rows, cols(h)])

    def Z3a(h):
        activate(h, 0)

    def Z3b(h):
        activate(h, 1)

    def B(h):
        arrive(h, "g0")
        arrive(h, "g1")

        def load(k):
            c = row_ref[k]
            return GG[h][c // 2, c % 2]
        products(tiles_t, load, COL_PREV)
        left(h, *GATHER)

        def place(core, b):
            def step(i, carry):
                for j in range(2):
                    k = i * 2 + j
                    G[h][k // 4, k % 4, core, b] = slots[plan[COL_LAST + k * 4 + core * 2 + b]]
                return carry
            lax.fori_loop(0, 8, step, 0)
        for b in range(2):
            place(q, b)
            send(G[h].at[:, :, q, b], R0[h].at[:, :, b], SIB, (h, "s" + str(b)))
        for b in range(2):
            place(p, b)

    def with_own(h, b):
        arrive(h, "s" + str(b))
        s = R0[h]

        def add(i, carry):
            s[i // 4, i % 4, b] = s[i // 4, i % 4, b] + G[h][i // 4, i % 4, p, b]
            return carry
        lax.fori_loop(0, 16, add, 0)

    def R1a(h):
        with_own(h, 0)
        s, m, f = R0[h], m1[h], f1[h]
        send(s.at[xo, :, 0, LO], m.at[0, 0], XR, (h, "m1"))
        send(s.at[xo, :, 0, HI], m.at[0, 1], XL, (h, "m1"))
        send(s.at[xr, :, 0, HI], f.at[0, 0, :, HI], XR, (h, "f1"))
        send(s.at[xl, :, 0, LO], f.at[0, 1, :, LO], XL, (h, "f1"))

    def R1b(h):
        with_own(h, 1)
        s, m, f = R0[h], m1[h], f1[h]
        send(s.at[:, yo, 1, LO], m.at[1, 0], YR, (h, "m1"))
        send(s.at[:, yo, 1, HI], m.at[1, 1], YL, (h, "m1"))
        send(s.at[:, yr, 1, HI], f.at[1, 0, :, HI], YR, (h, "f1"))
        send(s.at[:, yl, 1, LO], f.at[1, 1, :, LO], YL, (h, "f1"))

    def R2(h):
        s, m, f = R0[h], m1[h], f1[h]
        g = (h, "f1")
        arrive(h, "m1")
        s[xr, :, 0, LO] = s[xr, :, 0, LO] + m[0, 0]
        send(s.at[xr, :, 0, LO], f.at[0, 0, :, LO], XR, g)
        s[:, yr, 1, LO] = s[:, yr, 1, LO] + m[1, 0]
        send(s.at[:, yr, 1, LO], f.at[1, 0, :, LO], YR, g)
        s[xl, :, 0, HI] = s[xl, :, 0, HI] + m[0, 1]
        send(s.at[xl, :, 0, HI], f.at[0, 1, :, HI], XL, g)
        s[:, yl, 1, HI] = s[:, yl, 1, HI] + m[1, 1]
        send(s.at[:, yl, 1, HI], f.at[1, 1, :, HI], YL, g)

    def R3(h):
        arrive(h, "f1")
        s, f = R0[h], f1[h]
        f[0, 0] = f[0, 0] + f[0, 1] + s[x, :, 0]
        f[1, 0] = f[1, 0] + f[1, 1] + s[:, y, 1]
        t0, t1, m, b = f.at[0, 0], f.at[1, 0], m2[h], f2[h]
        g = (h, "f2")
        if h == C - 1:
            send(t0.at[yr], b.at[0, 0], YR, g)
            send(t1.at[xr], b.at[1, 0], XR, g)
            send(t0.at[yl], b.at[0, 1], YL, g)
            send(t1.at[xl], b.at[1, 1], XL, g)
            send(t0.at[yo], m.at[0], dev(dy=2), g)
            send(t1.at[xo], m.at[1], dev(dx=2), g)
            return
        send(t0.at[yo, LO], m.at[0, 0], YR, (h, "m2"))
        send(t1.at[xo, LO], m.at[1, 0], XR, (h, "m2"))
        send(t0.at[yo, HI], m.at[0, 1], YL, (h, "m2"))
        send(t1.at[xo, HI], m.at[1, 1], XL, (h, "m2"))
        send(t0.at[yr, HI], b.at[0, 0, HI], YR, g)
        send(t1.at[xr, HI], b.at[1, 0, HI], XR, g)
        send(t0.at[yl, LO], b.at[0, 1, LO], YL, g)
        send(t1.at[xl, LO], b.at[1, 1, LO], XL, g)

    def R4(h):
        if h == C - 1:
            return
        t, m, b = f1[h], m2[h], f2[h]
        arrive(h, "m2")
        for (i, j), rows, target, device in zip(
            ((0, 0), (1, 0), (0, 1), (1, 1)), (LO, LO, HI, HI), (yr, xr, yl, xl), (YR, XR, YL, XL)
        ):
            t[i, 0, target, rows] = t[i, 0, target, rows] + m[i, j]
            send(t.at[i, 0, target, rows], b.at[i, j, rows], device, (h, "f2"))

    def R5(h):
        arrive(h, "f2")
        t, g = f1[h], f2[h]
        own0, own1 = t[0, 0, y] + g[0, 0] + g[0, 1], t[1, 0, x] + g[1, 0] + g[1, 1]
        if h == C - 1:
            own0, own1 = own0 + m2[h][0], own1 + m2[h][1]
        prop[pl.ds(0, BLOCK), cols(h)] = own0
        prop[pl.ds(BLOCK, BLOCK), cols(h)] = own1
        right = split(prop[:, cols(h)])

        def weight_half(core):
            rows = pl.ds(pl.multiple_of(core * (PAD // 2), PAD // 2), PAD // 2)
            gwl[h][core] = mm((ft_hi[rows, :], ft_lo[rows, :]), right)
        weight_half(q)
        send(gwl[h].at[q], sb[h], SIB, (h, "w1"))
        weight_half(p)

    summed = []

    def grad_features(h):
        out = mm_nt(split(w_pad[:, cols(h)]), split(prop[:, cols(h)]))
        summed.append(h)
        if len(summed) == 1:
            gf_acc[...] = out
        else:
            gf_acc[...] = gf_acc[...] + out
        if len(summed) == C:
            gf[...] = gf_acc[pl.ds(0, F_IN), :]
            store(gf, gf_hbm)

    me = dict(x=x, y=y, z=z)

    def peers_of(axis):
        return [(at(me[axis], d), dev(**{"d" + axis: d})) for d in (1, 3, 2)]

    def groups(h):
        if h < C - 1:
            return [(0, PAD // 8, pl.ds(0, PAD // 8), "zxyz")]
        return [(0, 32, pl.ds(0, 32), "zxyz"), (128, 24, pl.ds(32, 24), "yzxy"), (224, 24, pl.ds(56, 24), "xyzx")]

    def piece(first, n, i):
        return pl.ds(pl.multiple_of(first + i * n, 8), n)

    def total(b, part_of):
        return (b[0, part_of] + b[1, part_of]) + (b[2, part_of] + b[3, part_of])

    def W2(h):
        arrive(h, "w1")
        sb[h][...] = sb[h][...] + gwl[h][p]
        for first, n, spot, axes in groups(h):
            mine = me[axes[0]]
            wa[h][mine, spot] = sb[h][piece(first, n, mine)]
            for i, device in peers_of(axes[0]):
                send(sb[h].at[piece(first, n, i)], wa[h].at[mine, spot], device, (h, "w2"))

    def exchange(h, before, after, source, target, step):
        arrive(h, before)
        for first, n, spot, axes in groups(h):
            mine = me[axes[step]]
            target[mine, spot] = total(source, spot)
            own = target.at[mine, spot]
            for i, device in peers_of(axes[step]):
                send(own, own, device, (h, after))

    def W3(h):
        exchange(h, "w2", "w3", wa[h], wb[h], 1)

    def W4(h):
        exchange(h, "w3", "w4", wb[h], wc[h], 2)

    def W5(h):
        arrive(h, "w4")
        for first, n, spot, axes in groups(h):
            rows = piece(first, n, me[axes[3]])
            gwo[h][p, rows] = total(wc[h], spot)
            own = gwo[h].at[p, rows]
            for i, device in peers_of(axes[3]):
                send(own, own, device, (h, "w5"))

    def W6(h):
        arrive(h, "w5")
        own = gwo[h].at[p]
        send(own, own, SIB, (h, "w6"))

    def W7(h):
        arrive(h, "w6")
        half = PAD // 2
        gw[pl.ds(0, half), cols(h)] = gwo[h][0]
        gw[pl.ds(half, F_IN - half), cols(h)] = gwo[h][1, pl.ds(0, F_IN - half)]
        store(gw.at[:, cols(h)], gw_hbm.at[:, cols(h)])

    stages = dict(P=project, A1=A1, A2=A2, A3=A3, A4=A4, A5=A5, F=F, Z1=Z1, Z3a=Z3a, Z3b=Z3b, B=B,
                  R1a=R1a, R1b=R1b, R2=R2, R3=R3, R4=R4, R5=R5, GF=grad_features, W2=W2, W3=W3, W4=W4, W5=W5, W6=W6, W7=W7)

    alone = dict(plan=link, turn=turn_tiles, ft=split_features, drain=drain)
    project(0)
    load_tiles.start()
    load_cot.start()
    pl.semaphore_wait(barrier, len(peers))
    for name in " ".join(ORDER).split()[1:]:
        if name in alone:
            alone[name]()
        else:
            stage, h = name.split("_")
            stages[stage](int(h))
    drain()
    for copy in stores:
        copy.wait()


ORDER = (
    "P_0 P_2 A1_2 ft",
    "P_1 A1_1 P_3 A2_2",
    "A1_0 A2_1 A3_2 A1_3",
    "plan turn A2_0 A4_2",
    "A3_0 A2_3 A5_2 F_2",
    "Z1_2 A4_0 A3_1 Z3a_2",
    "A5_0 Z3b_2 F_0 Z1_0",
    "A4_1 A3_3 B_2 Z3a_0",
    "A5_1 Z3b_0 F_1 Z1_1",
    "A4_3 R1a_2 R1b_2 B_0",
    "Z3a_1 A5_3 Z3b_1 R2_2",
    "R1b_0 R1a_0 F_3 Z1_3",
    "R3_2 B_1 Z3a_3 R2_0",
    "Z3b_3 R4_2 R1a_1 R1b_1",
    "R3_0 B_3 R2_1 R5_2",
    "GF_2 R4_0 R1a_3 R1b_3",
    "W2_2 R3_1 R5_0 GF_0",
    "W2_0 R2_3 R4_1 W3_0",
    "R3_3 R5_1 R4_3 GF_1",
    "W2_1 W4_0 W3_2 R5_3",
    "W3_1 W2_3 W4_2 W5_0",
    "GF_3 W3_3 W4_1 W5_2",
    "W6_0 drain W4_3 W7_0",
    "W5_1 W5_3 W6_2 W7_2",
    "W6_1 W6_3 W7_1 W7_3",
)


def hand_over(*refs):
    copies = [pltpu.make_async_copy(refs[i], refs[3 + i], refs[6].at[i]) for i in range(3)]
    for copy in copies:
        copy.start()
    for copy in copies:
        copy.wait()


def body(features, weight, cotangent, tile_values, tile_row, tile_col, tile_count):
    hidden = weight.shape[1]
    nodes, width = features.shape
    C = CHUNKS
    W = hidden // C

    def vmem(*shape, dtype=F32, count=C):
        return [pltpu.VMEM(shape, dtype)] * count

    scratch = (
        vmem(4, 4, 2, 2, BLOCK, W)
        + vmem(4, 4, 2, BLOCK, W)
        + vmem(4, 2, BLOCK, W)
        + vmem(3, 2, BLOCK, W)
        + vmem(4, 2, BLOCK, W)
        + vmem(2, 2, 4, HALF, W)
        + vmem(2, 2, 4, BLOCK, W)
        + vmem(2, 2, HALF, W, count=C - 1)
        + vmem(2, BLOCK, W, count=1)
        + vmem(2, 2, BLOCK, W)
        + vmem(2, PAD // 2, W)
        + vmem(PAD // 2, W)
        + vmem(4, PAD // 8, W)
        + vmem(4, PAD // 8, W)
        + vmem(4, PAD // 8, W)
        + vmem(2, PAD // 2, W)
        + [
            pltpu.VMEM((SLOTS + 1, BLOCK, W), F32),
            pltpu.VMEM((SLOTS, BLOCK, 2 * BLOCK), BF16),
            pltpu.VMEM((SLOTS, BLOCK, 2 * BLOCK), BF16),
            pltpu.VMEM((width, hidden), F32),
            pltpu.VMEM((PAD, hidden), F32),
            pltpu.VMEM((width, nodes), F32),
            pltpu.VMEM((nodes, hidden), F32),
            pltpu.VMEM((nodes, PAD), BF16),
            pltpu.VMEM((nodes, PAD), BF16),
            pltpu.VMEM((PAD, nodes), BF16),
            pltpu.VMEM((PAD, nodes), BF16),
            pltpu.VMEM((nodes, hidden), F32),
            pltpu.VMEM((PAD, nodes), F32),
            pltpu.SMEM((2 * SLOTS + ROWS + COLS,), jnp.int32),
            pltpu.VMEM((nodes, hidden), F32),
            pltpu.VMEM((width, nodes), F32),
            pltpu.VMEM((width, hidden), F32),
            pltpu.SemaphoreType.DMA((GROUPS * C,)),
            pltpu.SemaphoreType.DMA((GROUPS * C,)),
            pltpu.SemaphoreType.DMA((4,)),
            pltpu.SemaphoreType.DMA((3 * C + 1,)),
        ]
    )
    scalars = pl.BlockSpec(memory_space=pltpu.SMEM)
    hbm = pl.BlockSpec(memory_space=pl.ANY)
    shapes = (
        jax.ShapeDtypeStruct((nodes, hidden), F32),
        jax.ShapeDtypeStruct((width, nodes), F32),
        jax.ShapeDtypeStruct((width, hidden), F32),
    )
    results = pl.pallas_call(
        kernel,
        out_shape=shapes,
        in_specs=[scalars] * 3 + [hbm] * 4,
        out_specs=(hbm, hbm, hbm),
        scratch_shapes=scratch,
        compiler_params=pltpu.CompilerParams(
            collective_id=0, has_side_effects=True, vmem_limit_bytes=62 * 1024 * 1024),
    )(tile_row, tile_col, tile_count, features.T, weight, cotangent, tile_values)
    activated, grad_features, grad_weight = pl.pallas_call(
        hand_over,
        out_shape=shapes,
        in_specs=[pl.BlockSpec(memory_space=pltpu.VMEM)] * 3,
        out_specs=(hbm,) * 3,
        scratch_shapes=[pltpu.SemaphoreType.DMA((3,))],
    )(*results)
    return activated, grad_features.T, grad_weight


def solution(mesh):
    in_specs = (
        P(("rows", "rep"), None),
        P(),
        P(("rows", "rep"), None),
        P(("rows", "rep"), None, None),
        P(("rows", "rep")),
        P(("rows", "rep")),
        P(("rows", "rep")),
    )
    out_specs = (P(("rows", "rep"), None), P(("rows", "rep"), None), P())
    return jax.shard_map(body, mesh=mesh, in_specs=in_specs, out_specs=out_specs, check_vma=False)
```

```python
import functools
import math

import jax
import jax.numpy as jnp
from jax import lax
from jax.experimental import pallas as pl
from jax.experimental.pallas import tpu as pltpu
from jax.sharding import PartitionSpec as P

MESH = pl.DeviceIdType.MESH
F32 = jnp.float32
BF16 = jnp.bfloat16

BLOCK = 128
HALF = BLOCK // 2
SLOTS = 32
CHUNKS = 4
SIDE = 4
PAD = 640
GROUPS = 21

ROWS, COLS = 8, 64
ROW_PREV, ROW_LAST, COL_PREV, COL_LAST = 0, SLOTS, SLOTS + ROWS, 2 * SLOTS + ROWS

LO, HI = pl.ds(0, HALF), pl.ds(HALF, HALF)
POOLS = (("a1", "a2", "a3", "a4"), ("a5",), ("z0", "z1", "g0", "g1", "m2", "f2"), ("s0", "s1"), ("m1", "f1"),
         ("w1", "w2", "w3", "w4", "w5", "w6"))


def split(value):
    high = value.astype(BF16)
    return high, (value - high.astype(F32)).astype(BF16)


def mm(a, b):
    left = jnp.concatenate([a[0], a[1], a[0]], axis=1)
    right = jnp.concatenate([b[0], b[0], b[1]], axis=0)
    return jnp.dot(left, right, preferred_element_type=F32)


def mm_nt(a, b):
    left = jnp.concatenate([a[0], a[1], a[0]], axis=1)
    right = jnp.concatenate([b[0], b[0], b[1]], axis=1)
    return lax.dot_general(left, right, (((1,), (1,)), ((), ())), preferred_element_type=F32)


def kernel(*refs):
    C = CHUNKS
    row_ref, col_ref, live_ref, f_hbm, w_hbm, cot_hbm, tiles_hbm, act_hbm, gf_hbm, gw_hbm = refs[:10]
    refs = list(refs[10:])

    def take(count):
        out = refs[:count]
        del refs[:count]
        return out

    G, R0, part, zfin, GG = (take(C) for _ in range(5))
    m1, f1, m2, f2 = (take(C) for _ in range(4))
    gwl, sb, wa, wb, wc, gwo = (take(C) for _ in range(6))
    slots, tiles, tiles_t, w_raw, w_pad, f_raw, cot, f_hi, f_lo, ft_hi, ft_lo, prop, gf_acc, plan = take(14)
    act, gf, gw = take(3)
    send_sem, recv_sem, load_sem, store_sem = take(4)
    W = prop.shape[1] // C

    r = lax.axis_index("rows")
    z = lax.axis_index("rep")
    x, y, p = r // 8, (r // 2) % 4, r % 2
    q = 1 - p

    def at(i, d):
        return (i + d) % SIDE

    def dev(dx=0, dy=0, dz=0, core=None):
        c = p if core is None else core
        return (at(x, dx) * 8 + at(y, dy) * 2 + c, at(z, dz))

    xl, xr, xo = at(x, 3), at(x, 1), at(x, 2)
    yl, yr, yo = at(y, 3), at(y, 1), at(y, 2)
    zl, zr, zo = at(z, 3), at(z, 1), at(z, 2)
    XR, XL, YR, YL, ZR, ZL = dev(dx=1), dev(dx=3), dev(dy=1), dev(dy=3), dev(dz=1), dev(dz=3)
    SIB = dev(core=q)

    stores = []

    def store(src, dst):
        copy = pltpu.make_async_copy(src, dst, store_sem.at[len(stores)])
        copy.start()
        stores.append(copy)

    ready = []

    def need(load):
        if not any(load is other for other in ready):
            load.wait()
            ready.append(load)

    names = [[] for _ in range(C)]
    lines = {}
    gone = {}

    def spot(group):
        chunk, name = group
        if name not in names[chunk]:
            names[chunk].append(name)
        return GROUPS * chunk + names[chunk].index(name)

    def pool(group):
        chunk, name = group
        return len(POOLS) * chunk + [name in names_of for names_of in POOLS].index(True)

    def send(src, dst, device, group):
        copy = pltpu.make_async_remote_copy(
            src_ref=src, dst_ref=dst, send_sem=send_sem.at[pool(group)], recv_sem=recv_sem.at[spot(group)],
            device_id=device, device_id_type=MESH)
        copy.start()
        count = math.prod(src.shape) // W
        lines[group] = lines.get(group, 0) + count
        gone[pool(group)] = gone.get(pool(group), 0) + count

    def all_of(count, sent, received):
        blocks = count // BLOCK
        if blocks * BLOCK == count:
            ref = slots.at[pl.ds(0, blocks)]
        elif count <= PAD // 2:
            ref = sb[0].at[pl.ds(0, count)]
        else:
            ref = w_pad.at[pl.ds(0, count // C)]
        return pltpu.make_async_remote_copy(
            src_ref=ref, dst_ref=ref, send_sem=send_sem.at[sent], recv_sem=recv_sem.at[received],
            device_id=XR, device_id_type=MESH)

    def arrive(*group):
        all_of(lines[group], pool(group), spot(group)).wait_recv()

    def left(h, *which):
        for number in which:
            i = len(POOLS) * h + number
            all_of(gone[i], i, 0).wait_send()

    def drain():
        for h in range(C):
            left(h, 2, 3, 4)

    loads = [
        pltpu.make_async_copy(src, dst, load_sem.at[i])
        for i, (src, dst) in enumerate(
            [(f_hbm, f_raw), (cot_hbm, cot), (tiles_hbm, slots.at[pl.ds(0, SLOTS)])]
            + [(w_hbm.at[:, pl.ds(h * W, W)], w_raw.at[:, pl.ds(h * W, W)]) for h in range(C)])
    ]
    load_f, load_cot, load_tiles = loads[:3]
    load_w = loads[3:]
    load_f.start()
    for load in load_w:
        load.start()

    barrier = pltpu.get_barrier_semaphore()
    peers = [dev(dx=d) for d in (1, 2, 3)] + [dev(dy=d) for d in (1, 2, 3)] + [dev(dz=d) for d in (1, 2, 3)] + [SIB]
    for peer in peers:
        pl.semaphore_signal(barrier, inc=1, device_id=peer, device_id_type=MESH)

    F_IN = f_hbm.shape[0]
    tail = F_IN // 8 * 8
    ft_pad = gf_acc
    load_f.wait()
    ft_pad[pl.ds(tail, PAD - tail), :] = jnp.zeros((PAD - tail, ft_pad.shape[1]), F32)
    ft_pad[pl.ds(0, F_IN), :] = f_raw[...]
    f_hi[...], f_lo[...] = split(ft_pad[...].T)

    def cols(h):
        return pl.ds(h * W, W)

    def project(h):
        need(load_w[h])
        w_pad[pl.ds(tail, PAD - tail), cols(h)] = jnp.zeros((PAD - tail, W), F32)
        w_pad[pl.ds(0, F_IN), cols(h)] = w_raw[:, cols(h)]
        out = mm((f_hi[...], f_lo[...]), split(w_pad[:, cols(h)]))
        G[h][x, y, p, 0] = out[:BLOCK]
        G[h][x, y, p, 1] = out[BLOCK:]

    def A1(h):
        own0, own1 = G[h].at[x, y, p, 0], G[h].at[x, y, p, 1]
        g = (h, "a1")
        for ref, device in ((own0, XR), (own0, XL), (own1, YR), (own1, YL)):
            send(ref, ref, device, g)

    def A2(h):
        arrive(h, "a1")
        for ref, device in (
            (G[h].at[xl, y, p, 0, LO], XR), (G[h].at[xr, y, p, 0, HI], XL),
            (G[h].at[x, yl, p, 1, LO], YR), (G[h].at[x, yr, p, 1, HI], YL),
        ):
            send(ref, ref, device, (h, "a2"))

    def A3(h):
        arrive(h, "a2")
        line0, line1 = G[h].at[:, y, p, 0], G[h].at[x, :, p, 1]
        for line, device in ((line0, YR), (line1, XR), (line0, YL), (line1, XL)):
            send(line, line, device, (h, "a3"))
        for line in (line0, line1):
            send(line, line, SIB, (h, "a5"))

    def A4(h):
        arrive(h, "a3")
        for ref, device in (
            (G[h].at[:, yl, p, 0, LO], YR), (G[h].at[xl, :, p, 1, LO], XR),
            (G[h].at[:, yr, p, 0, HI], YL), (G[h].at[xr, :, p, 1, HI], XL),
        ):
            send(ref, ref, device, (h, "a4"))
        for line in (G[h].at[:, yl, p, 0], G[h].at[xl, :, p, 1], G[h].at[:, yr, p, 0], G[h].at[xr, :, p, 1]):
            send(line, line, SIB, (h, "a5"))

    def A5(h):
        arrive(h, "a4")
        for line in (G[h].at[:, yo, p, 0], G[h].at[xo, :, p, 1]):
            send(line, line, SIB, (h, "a5"))

    def products(left_ref, load, prev):
        def product(k):
            both = left_ref[k]
            return mm((both[:, :BLOCK], both[:, BLOCK:]), split(load(k)))

        def add(i):
            for j in range(4):
                k = i * 4 + j
                slots[k] = slots[k] + slots[plan[prev + k]]

        def put(i, out):
            for j in range(4):
                slots[i * 4 + j] = out[j]

        def step(i, carry):
            out = [product(i * 4 + j) for j in range(4)]
            add(i - 1)
            put(i, out)
            return carry
        put(0, [product(j) for j in range(4)])
        lax.fori_loop(1, SLOTS // 4, step, 0)
        add(SLOTS // 4 - 1)

    def link_slots():
        lane = lax.broadcasted_iota(jnp.int32, (1, 128), 1)
        live = live_ref[0]
        for index, targets, prev, last in ((row_ref, ROWS, ROW_PREV, ROW_LAST), (col_ref, COLS, COL_PREV, COL_LAST)):
            held = jnp.full((1, 128), -1, jnp.int32)
            for k in range(SLOTS):
                held = jnp.where(lane == k, index[k], held)
            held = jnp.where(lane < live, held, -1)

            def find(match):
                best = jnp.max(jnp.where(match, lane, -1))
                return jnp.where(best < 0, SLOTS, best)

            def before(i, carry):
                for j in range(8):
                    k = i * 8 + j
                    plan[prev + k] = find((held == index[k]) & (lane < k))
                return carry
            lax.fori_loop(0, SLOTS // 8, before, 0)

            def final(i, carry):
                for j in range(8):
                    k = i * 8 + j
                    plan[last + k] = find(held == k)
                return carry
            lax.fori_loop(0, targets // 8, final, 0)

    def link():
        slots[SLOTS] = jnp.zeros(slots.shape[1:], F32)
        link_slots()

    def turn_tiles():
        def turn(k, carry):
            tile = slots[k]
            tiles[k] = jnp.concatenate(split(tile), axis=1)
            tiles_t[k] = jnp.concatenate(split(tile.T), axis=1)
            return carry
        need(load_tiles)
        lax.fori_loop(0, SLOTS, turn, 0, unroll=4)

    def split_features():
        ft_hi[...], ft_lo[...] = split(ft_pad[...])

    def F(h):
        arrive(h, "a5")

        def load(k):
            c = col_ref[k]
            return G[h][c // 16, (c // 4) % 4, (c // 2) % 2, c % 2]
        products(tiles, load, ROW_PREV)
        for i in range(2 * SIDE):
            part[h][i // 2, i % 2] = slots[plan[ROW_LAST + i]]

    def Z1(h):
        for b in range(2):
            for d in (1, 3, 2):
                send(part[h].at[at(z, d), b], zfin[h].at[d - 1, b], dev(dz=d), (h, "z" + str(b)))

    def activate(h, b):
        arrive(h, "z" + str(b))
        need(load_cot)
        rows = pl.ds(b * BLOCK, BLOCK)
        s = (part[h][z, b] + zfin[h][0, b]) + (zfin[h][1, b] + zfin[h][2, b])
        sigma = jax.nn.sigmoid(s)
        act[rows, cols(h)] = s * sigma
        GG[h][z, b] = cot[rows, cols(h)] * sigma * (1.0 + s * (1.0 - sigma))
        own = GG[h].at[z, b]
        for d in (1, 3, 2):
            send(own, own, dev(dz=d), (h, "g" + str(b)))
        store(act.at[rows, cols(h)], act_hbm.at[rows, cols(h)])

    def Z3a(h):
        activate(h, 0)

    def Z3b(h):
        activate(h, 1)

    def B(h):
        arrive(h, "g0")
        arrive(h, "g1")

        def load(k):
            c = row_ref[k]
            return GG[h][c // 2, c % 2]
        products(tiles_t, load, COL_PREV)
        left(h, 0, 1)

        def place(core, b):
            def step(i, carry):
                for j in range(2):
                    k = i * 2 + j
                    G[h][k // 4, k % 4, core, b] = slots[plan[COL_LAST + k * 4 + core * 2 + b]]
                return carry
            lax.fori_loop(0, 8, step, 0)
        for b in range(2):
            place(q, b)
            send(G[h].at[:, :, q, b], R0[h].at[:, :, b], SIB, (h, "s" + str(b)))
        for b in range(2):
            place(p, b)

    def with_own(h, b):
        arrive(h, "s" + str(b))
        s = R0[h]

        def add(i, carry):
            s[i // 4, i % 4, b] = s[i // 4, i % 4, b] + G[h][i // 4, i % 4, p, b]
            return carry
        lax.fori_loop(0, 16, add, 0, unroll=4)

    def R1a(h):
        with_own(h, 0)
        s, m, f = R0[h], m1[h], f1[h]
        send(s.at[xo, :, 0, LO], m.at[0, 0], XR, (h, "m1"))
        send(s.at[xo, :, 0, HI], m.at[0, 1], XL, (h, "m1"))
        send(s.at[xr, :, 0, HI], f.at[0, 0, :, HI], XR, (h, "f1"))
        send(s.at[xl, :, 0, LO], f.at[0, 1, :, LO], XL, (h, "f1"))

    def R1b(h):
        with_own(h, 1)
        s, m, f = R0[h], m1[h], f1[h]
        send(s.at[:, yo, 1, LO], m.at[1, 0], YR, (h, "m1"))
        send(s.at[:, yo, 1, HI], m.at[1, 1], YL, (h, "m1"))
        send(s.at[:, yr, 1, HI], f.at[1, 0, :, HI], YR, (h, "f1"))
        send(s.at[:, yl, 1, LO], f.at[1, 1, :, LO], YL, (h, "f1"))

    def R2(h):
        s, m, f = R0[h], m1[h], f1[h]
        g = (h, "f1")
        arrive(h, "m1")
        s[xr, :, 0, LO] = s[xr, :, 0, LO] + m[0, 0]
        send(s.at[xr, :, 0, LO], f.at[0, 0, :, LO], XR, g)
        s[:, yr, 1, LO] = s[:, yr, 1, LO] + m[1, 0]
        send(s.at[:, yr, 1, LO], f.at[1, 0, :, LO], YR, g)
        s[xl, :, 0, HI] = s[xl, :, 0, HI] + m[0, 1]
        send(s.at[xl, :, 0, HI], f.at[0, 1, :, HI], XL, g)
        s[:, yl, 1, HI] = s[:, yl, 1, HI] + m[1, 1]
        send(s.at[:, yl, 1, HI], f.at[1, 1, :, HI], YL, g)

    def R3(h):
        arrive(h, "f1")
        s, f = R0[h], f1[h]
        f[0, 0] = f[0, 0] + f[0, 1] + s[x, :, 0]
        f[1, 0] = f[1, 0] + f[1, 1] + s[:, y, 1]
        t0, t1, m, b = f.at[0, 0], f.at[1, 0], m2[h], f2[h]
        g = (h, "f2")
        if h == C - 1:
            send(t0.at[yr], b.at[0, 0], YR, g)
            send(t1.at[xr], b.at[1, 0], XR, g)
            send(t0.at[yl], b.at[0, 1], YL, g)
            send(t1.at[xl], b.at[1, 1], XL, g)
            send(t0.at[yo], m.at[0], dev(dy=2), g)
            send(t1.at[xo], m.at[1], dev(dx=2), g)
            return
        send(t0.at[yo, LO], m.at[0, 0], YR, (h, "m2"))
        send(t1.at[xo, LO], m.at[1, 0], XR, (h, "m2"))
        send(t0.at[yo, HI], m.at[0, 1], YL, (h, "m2"))
        send(t1.at[xo, HI], m.at[1, 1], XL, (h, "m2"))
        send(t0.at[yr, HI], b.at[0, 0, HI], YR, g)
        send(t1.at[xr, HI], b.at[1, 0, HI], XR, g)
        send(t0.at[yl, LO], b.at[0, 1, LO], YL, g)
        send(t1.at[xl, LO], b.at[1, 1, LO], XL, g)

    def R4(h):
        if h == C - 1:
            return
        t, m, b = f1[h], m2[h], f2[h]
        arrive(h, "m2")
        for (i, j), rows, target, device in zip(
            ((0, 0), (1, 0), (0, 1), (1, 1)), (LO, LO, HI, HI), (yr, xr, yl, xl), (YR, XR, YL, XL)
        ):
            t[i, 0, target, rows] = t[i, 0, target, rows] + m[i, j]
            send(t.at[i, 0, target, rows], b.at[i, j, rows], device, (h, "f2"))

    def R5(h):
        arrive(h, "f2")
        t, g = f1[h], f2[h]
        own0, own1 = t[0, 0, y] + g[0, 0] + g[0, 1], t[1, 0, x] + g[1, 0] + g[1, 1]
        if h == C - 1:
            own0, own1 = own0 + m2[h][0], own1 + m2[h][1]
        prop[pl.ds(0, BLOCK), cols(h)] = own0
        prop[pl.ds(BLOCK, BLOCK), cols(h)] = own1
        right = split(prop[:, cols(h)])

        def weight_half(core):
            rows = pl.ds(pl.multiple_of(core * (PAD // 2), PAD // 2), PAD // 2)
            gwl[h][core] = mm((ft_hi[rows, :], ft_lo[rows, :]), right)
        weight_half(q)
        send(gwl[h].at[q], sb[h], SIB, (h, "w1"))
        weight_half(p)

    summed = []

    def grad_features(h):
        out = mm_nt(split(w_pad[:, cols(h)]), split(prop[:, cols(h)]))
        summed.append(h)
        if len(summed) == 1:
            gf_acc[...] = out
        else:
            gf_acc[...] = gf_acc[...] + out
        if len(summed) == C:
            gf[...] = gf_acc[pl.ds(0, F_IN), :]
            store(gf, gf_hbm)

    me = dict(x=x, y=y, z=z)

    def peers_of(axis):
        return [(at(me[axis], d), dev(**{"d" + axis: d})) for d in (1, 3, 2)]

    def groups(h):
        if h < C - 1:
            return [(0, PAD // 8, pl.ds(0, PAD // 8), "zxyz")]
        return [(0, 32, pl.ds(0, 32), "zxyz"), (128, 24, pl.ds(32, 24), "yzxy"), (224, 24, pl.ds(56, 24), "xyzx")]

    def piece(first, n, i):
        return pl.ds(pl.multiple_of(first + i * n, 8), n)

    def total(b, part_of):
        return (b[0, part_of] + b[1, part_of]) + (b[2, part_of] + b[3, part_of])

    def W2(h):
        arrive(h, "w1")
        sb[h][...] = sb[h][...] + gwl[h][p]
        for first, n, spot, axes in groups(h):
            mine = me[axes[0]]
            wa[h][mine, spot] = sb[h][piece(first, n, mine)]
            for i, device in peers_of(axes[0]):
                send(sb[h].at[piece(first, n, i)], wa[h].at[mine, spot], device, (h, "w2"))

    def exchange(h, before, after, source, target, step):
        arrive(h, before)
        for first, n, spot, axes in groups(h):
            mine = me[axes[step]]
            target[mine, spot] = total(source, spot)
            own = target.at[mine, spot]
            for i, device in peers_of(axes[step]):
                send(own, own, device, (h, after))

    def W3(h):
        exchange(h, "w2", "w3", wa[h], wb[h], 1)

    def W4(h):
        exchange(h, "w3", "w4", wb[h], wc[h], 2)

    def W5(h):
        arrive(h, "w4")
        for first, n, spot, axes in groups(h):
            rows = piece(first, n, me[axes[3]])
            gwo[h][p, rows] = total(wc[h], spot)
            own = gwo[h].at[p, rows]
            for i, device in peers_of(axes[3]):
                send(own, own, device, (h, "w5"))

    def W6(h):
        arrive(h, "w5")
        own = gwo[h].at[p]
        send(own, own, SIB, (h, "w6"))

    def W7(h):
        arrive(h, "w6")
        half = PAD // 2
        gw[pl.ds(0, half), cols(h)] = gwo[h][0]
        gw[pl.ds(half, F_IN - half), cols(h)] = gwo[h][1, pl.ds(0, F_IN - half)]
        store(gw.at[:, cols(h)], gw_hbm.at[:, cols(h)])

    stages = dict(P=project, A1=A1, A2=A2, A3=A3, A4=A4, A5=A5, F=F, Z1=Z1, Z3a=Z3a, Z3b=Z3b, B=B,
                  R1a=R1a, R1b=R1b, R2=R2, R3=R3, R4=R4, R5=R5, GF=grad_features, W2=W2, W3=W3, W4=W4, W5=W5, W6=W6, W7=W7)

    alone = dict(plan=link, turn=turn_tiles, ft=split_features, drain=drain)
    project(0)
    load_tiles.start()
    load_cot.start()
    pl.semaphore_wait(barrier, len(peers))
    for name in " ".join(ORDER).split()[1:]:
        if name in alone:
            alone[name]()
        else:
            stage, h = name.split("_")
            stages[stage](int(h))
    for h in range(C):
        left(h, 5)
    for copy in stores:
        copy.wait()


ORDER = (
    "P_0 A1_0 P_1 ft",
    "A1_1 P_2 P_3 turn",
    "A2_0 A1_2 A3_0 A2_1",
    "plan A2_2 A4_0 A3_1",
    "A5_0 A1_3 F_0 Z1_0",
    "A4_1 A3_2 Z3a_0 A5_1",
    "A2_3 Z3b_0 F_1 Z1_1",
    "A4_2 A3_3 B_0 Z3a_1",
    "A5_2 Z3b_1 F_2 Z1_2",
    "A4_3 R1b_0 R1a_0 B_1",
    "A5_3 Z3a_2 Z3b_2 R2_0",
    "R1a_1 R1b_1 F_3 Z1_3",
    "B_2 R3_0 R2_1 Z3a_3",
    "Z3b_3 R4_0 R1a_2 R1b_2",
    "R3_1 R5_0 B_3 R2_2",
    "W2_0 R4_1 GF_0 R1a_3",
    "R1b_3 R3_2 R5_1 GF_1",
    "W2_1 R2_3 W3_0 R4_2",
    "R3_3 W3_1 R5_2 W4_0",
    "W2_2 R5_3 W2_3 W3_2",
    "W4_1 W5_0 GF_2 W3_3",
    "W4_2 W5_1 drain W4_3",
    "W5_2 W6_1 GF_3 R4_3",
    "W5_3 W7_1 W6_2 W6_0",
    "W6_3 W7_2 W7_0 W7_3",
)


def hand_over(*refs):
    copies = [pltpu.make_async_copy(refs[i], refs[3 + i], refs[6].at[i]) for i in range(3)]
    for copy in copies:
        copy.start()
    for copy in copies:
        copy.wait()


def body(features, weight, cotangent, tile_values, tile_row, tile_col, tile_count):
    hidden = weight.shape[1]
    nodes, width = features.shape
    C = CHUNKS
    W = hidden // C

    def vmem(*shape, dtype=F32, count=C):
        return [pltpu.VMEM(shape, dtype)] * count

    scratch = (
        vmem(4, 4, 2, 2, BLOCK, W)
        + vmem(4, 4, 2, BLOCK, W)
        + vmem(4, 2, BLOCK, W)
        + vmem(3, 2, BLOCK, W)
        + vmem(4, 2, BLOCK, W)
        + vmem(2, 2, 4, HALF, W)
        + vmem(2, 2, 4, BLOCK, W)
        + vmem(2, 2, HALF, W, count=C - 1)
        + vmem(2, BLOCK, W, count=1)
        + vmem(2, 2, BLOCK, W)
        + vmem(2, PAD // 2, W)
        + vmem(PAD // 2, W)
        + vmem(4, PAD // 8, W)
        + vmem(4, PAD // 8, W)
        + vmem(4, PAD // 8, W)
        + vmem(2, PAD // 2, W)
        + [
            pltpu.VMEM((SLOTS + 1, BLOCK, W), F32),
            pltpu.VMEM((SLOTS, BLOCK, 2 * BLOCK), BF16),
            pltpu.VMEM((SLOTS, BLOCK, 2 * BLOCK), BF16),
            pltpu.VMEM((width, hidden), F32),
            pltpu.VMEM((PAD, hidden), F32),
            pltpu.VMEM((width, nodes), F32),
            pltpu.VMEM((nodes, hidden), F32),
            pltpu.VMEM((nodes, PAD), BF16),
            pltpu.VMEM((nodes, PAD), BF16),
            pltpu.VMEM((PAD, nodes), BF16),
            pltpu.VMEM((PAD, nodes), BF16),
            pltpu.VMEM((nodes, hidden), F32),
            pltpu.VMEM((PAD, nodes), F32),
            pltpu.SMEM((2 * SLOTS + ROWS + COLS,), jnp.int32),
            pltpu.VMEM((nodes, hidden), F32),
            pltpu.VMEM((width, nodes), F32),
            pltpu.VMEM((width, hidden), F32),
            pltpu.SemaphoreType.DMA((len(POOLS) * C,)),
            pltpu.SemaphoreType.DMA((GROUPS * C,)),
            pltpu.SemaphoreType.DMA((3 + C,)),
            pltpu.SemaphoreType.DMA((3 * C + 1,)),
        ]
    )
    scalars = pl.BlockSpec(memory_space=pltpu.SMEM)
    hbm = pl.BlockSpec(memory_space=pl.ANY)
    shapes = (
        jax.ShapeDtypeStruct((nodes, hidden), F32),
        jax.ShapeDtypeStruct((width, nodes), F32),
        jax.ShapeDtypeStruct((width, hidden), F32),
    )
    results = pl.pallas_call(
        kernel,
        out_shape=shapes,
        in_specs=[scalars] * 3 + [hbm] * 4,
        out_specs=(hbm, hbm, hbm),
        scratch_shapes=scratch,
        compiler_params=pltpu.CompilerParams(
            collective_id=0, has_side_effects=True, vmem_limit_bytes=62 * 1024 * 1024),
    )(tile_row, tile_col, tile_count, features.T, weight, cotangent, tile_values)
    activated, grad_features, grad_weight = pl.pallas_call(
        hand_over,
        out_shape=shapes,
        in_specs=[pl.BlockSpec(memory_space=pltpu.VMEM)] * 3,
        out_specs=(hbm,) * 3,
        scratch_shapes=[pltpu.SemaphoreType.DMA((3,))],
    )(*results)
    return activated, grad_features.T, grad_weight


def solution(mesh):
    in_specs = (
        P(("rows", "rep"), None),
        P(),
        P(("rows", "rep"), None),
        P(("rows", "rep"), None, None),
        P(("rows", "rep")),
        P(("rows", "rep")),
        P(("rows", "rep")),
    )
    out_specs = (P(("rows", "rep"), None), P(("rows", "rep"), None), P())
    return jax.shard_map(body, mesh=mesh, in_specs=in_specs, out_specs=out_specs, check_vma=False)
```

```python
import functools
import math

import jax
import jax.numpy as jnp
from jax import lax
from jax.experimental import pallas as pl
from jax.experimental.pallas import tpu as pltpu
from jax.sharding import PartitionSpec as P

MESH = pl.DeviceIdType.MESH
F32 = jnp.float32
BF16 = jnp.bfloat16

BLOCK = 128
HALF = BLOCK // 2
SLOTS = 32
CHUNKS = 4
SIDE = 4
PAD = 640
GROUPS = 21

ROWS, COLS = 8, 64
ROW_PREV, ROW_LAST, COL_PREV, COL_LAST = 0, SLOTS, SLOTS + ROWS, 2 * SLOTS + ROWS

LO, HI = pl.ds(0, HALF), pl.ds(HALF, HALF)
POOLS = (("a1", "a2", "a3", "a4"), ("a5",), ("z0", "z1", "g0", "g1", "m2", "f2"), ("s0", "s1"), ("m1", "f1"),
         ("w1", "w2", "w3", "w4", "w5", "w6"))


def split(value):
    high = value.astype(BF16)
    return high, (value - high.astype(F32)).astype(BF16)


def mm(a, b):
    left = jnp.concatenate([a[0], a[1], a[0]], axis=1)
    right = jnp.concatenate([b[0], b[0], b[1]], axis=0)
    return jnp.dot(left, right, preferred_element_type=F32)


def mm_nt(a, b):
    left = jnp.concatenate([a[0], a[1], a[0]], axis=1)
    right = jnp.concatenate([b[0], b[0], b[1]], axis=1)
    return lax.dot_general(left, right, (((1,), (1,)), ((), ())), preferred_element_type=F32)


def kernel(*refs):
    C = CHUNKS
    row_ref, col_ref, live_ref, f_hbm, w_hbm, cot_hbm, tiles_hbm, act_hbm, gf_hbm, gw_hbm = refs[:10]
    refs = list(refs[10:])

    def take(count):
        out = refs[:count]
        del refs[:count]
        return out

    G, R0, part, zfin, GG = (take(C) for _ in range(5))
    m1, f1, m2, f2 = (take(C) for _ in range(4))
    gwl, sb, wa, wb, wc, gwo = (take(C) for _ in range(6))
    slots, tiles, tiles_t, w_raw, w_pad, f_raw, cot, f_hi, f_lo, ft_hi, ft_lo, prop, gf_acc, plan = take(14)
    act, gf, gw = take(3)
    send_sem, recv_sem, load_sem, store_sem = take(4)
    W = prop.shape[1] // C

    r = lax.axis_index("rows")
    z = lax.axis_index("rep")
    x, y, p = r // 8, (r // 2) % 4, r % 2
    q = 1 - p

    def at(i, d):
        return (i + d) % SIDE

    def dev(dx=0, dy=0, dz=0, core=None):
        c = p if core is None else core
        return (at(x, dx) * 8 + at(y, dy) * 2 + c, at(z, dz))

    xl, xr, xo = at(x, 3), at(x, 1), at(x, 2)
    yl, yr, yo = at(y, 3), at(y, 1), at(y, 2)
    zl, zr, zo = at(z, 3), at(z, 1), at(z, 2)
    XR, XL, YR, YL, ZR, ZL = dev(dx=1), dev(dx=3), dev(dy=1), dev(dy=3), dev(dz=1), dev(dz=3)
    SIB = dev(core=q)

    stores = []

    def store(src, dst):
        copy = pltpu.make_async_copy(src, dst, store_sem.at[len(stores)])
        copy.start()
        stores.append(copy)

    ready = []

    def need(load):
        if not any(load is other for other in ready):
            load.wait()
            ready.append(load)

    names = [[] for _ in range(C)]
    lines = {}
    gone = {}

    def spot(group):
        chunk, name = group
        if name not in names[chunk]:
            names[chunk].append(name)
        return GROUPS * chunk + names[chunk].index(name)

    def pool(group):
        chunk, name = group
        return len(POOLS) * chunk + [name in names_of for names_of in POOLS].index(True)

    def send(src, dst, device, group):
        copy = pltpu.make_async_remote_copy(
            src_ref=src, dst_ref=dst, send_sem=send_sem.at[pool(group)], recv_sem=recv_sem.at[spot(group)],
            device_id=device, device_id_type=MESH)
        copy.start()
        count = math.prod(src.shape) // W
        lines[group] = lines.get(group, 0) + count
        gone[pool(group)] = gone.get(pool(group), 0) + count

    def all_of(count, sent, received):
        blocks = count // BLOCK
        if blocks * BLOCK == count:
            ref = slots.at[pl.ds(0, blocks)]
        elif count <= PAD // 2:
            ref = sb[0].at[pl.ds(0, count)]
        else:
            ref = w_pad.at[pl.ds(0, count // C)]
        return pltpu.make_async_remote_copy(
            src_ref=ref, dst_ref=ref, send_sem=send_sem.at[sent], recv_sem=recv_sem.at[received],
            device_id=XR, device_id_type=MESH)

    def arrive(*group):
        all_of(lines[group], pool(group), spot(group)).wait_recv()

    def left(h, *which):
        for number in which:
            i = len(POOLS) * h + number
            all_of(gone[i], i, 0).wait_send()

    def drain():
        for h in range(C):
            left(h, 2, 3, 4)

    loads = [
        pltpu.make_async_copy(src, dst, load_sem.at[i])
        for i, (src, dst) in enumerate(
            [(f_hbm, f_raw), (cot_hbm, cot), (tiles_hbm, slots.at[pl.ds(0, SLOTS)])]
            + [(w_hbm.at[:, pl.ds(h * W, W)], w_raw.at[:, pl.ds(h * W, W)]) for h in range(C)])
    ]
    load_f, load_cot, load_tiles = loads[:3]
    load_w = loads[3:]
    load_f.start()
    for load in load_w:
        load.start()

    barrier = pltpu.get_barrier_semaphore()
    peers = [dev(dx=d) for d in (1, 2, 3)] + [dev(dy=d) for d in (1, 2, 3)] + [dev(dz=d) for d in (1, 2, 3)] + [SIB]
    for peer in peers:
        pl.semaphore_signal(barrier, inc=1, device_id=peer, device_id_type=MESH)

    F_IN = f_hbm.shape[0]
    tail = F_IN // 8 * 8
    ft_pad = gf_acc
    load_f.wait()
    ft_pad[pl.ds(tail, PAD - tail), :] = jnp.zeros((PAD - tail, ft_pad.shape[1]), F32)
    ft_pad[pl.ds(0, F_IN), :] = f_raw[...]
    f_hi[...], f_lo[...] = split(ft_pad[...].T)

    def cols(h):
        return pl.ds(h * W, W)

    def project(h):
        need(load_w[h])
        w_pad[pl.ds(tail, PAD - tail), cols(h)] = jnp.zeros((PAD - tail, W), F32)
        w_pad[pl.ds(0, F_IN), cols(h)] = w_raw[:, cols(h)]
        out = mm((f_hi[...], f_lo[...]), split(w_pad[:, cols(h)]))
        G[h][x, y, p, 0] = out[:BLOCK]
        G[h][x, y, p, 1] = out[BLOCK:]

    def A1(h):
        own0, own1 = G[h].at[x, y, p, 0], G[h].at[x, y, p, 1]
        g = (h, "a1")
        for ref, device in ((own0, XR), (own0, XL), (own1, YR), (own1, YL)):
            send(ref, ref, device, g)

    def A2(h):
        arrive(h, "a1")
        for ref, device in (
            (G[h].at[xl, y, p, 0, LO], XR), (G[h].at[xr, y, p, 0, HI], XL),
            (G[h].at[x, yl, p, 1, LO], YR), (G[h].at[x, yr, p, 1, HI], YL),
        ):
            send(ref, ref, device, (h, "a2"))

    def A3(h):
        arrive(h, "a2")
        line0, line1 = G[h].at[:, y, p, 0], G[h].at[x, :, p, 1]
        for line, device in ((line0, YR), (line1, XR), (line0, YL), (line1, XL)):
            send(line, line, device, (h, "a3"))
        for line in (line0, line1):
            send(line, line, SIB, (h, "a5"))

    def A4(h):
        arrive(h, "a3")
        for ref, device in (
            (G[h].at[:, yl, p, 0, LO], YR), (G[h].at[xl, :, p, 1, LO], XR),
            (G[h].at[:, yr, p, 0, HI], YL), (G[h].at[xr, :, p, 1, HI], XL),
        ):
            send(ref, ref, device, (h, "a4"))
        for line in (G[h].at[:, yl, p, 0], G[h].at[xl, :, p, 1], G[h].at[:, yr, p, 0], G[h].at[xr, :, p, 1]):
            send(line, line, SIB, (h, "a5"))

    def A5(h):
        arrive(h, "a4")
        for line in (G[h].at[:, yo, p, 0], G[h].at[xo, :, p, 1]):
            send(line, line, SIB, (h, "a5"))

    def products(left_ref, load, prev):
        def product(k):
            both = left_ref[k]
            return mm((both[:, :BLOCK], both[:, BLOCK:]), split(load(k)))

        def add(i):
            for j in range(4):
                k = i * 4 + j
                slots[k] = slots[k] + slots[plan[prev + k]]

        def put(i, out):
            for j in range(4):
                slots[i * 4 + j] = out[j]

        def step(i, carry):
            out = [product(i * 4 + j) for j in range(4)]
            add(i - 1)
            put(i, out)
            return carry
        put(0, [product(j) for j in range(4)])
        lax.fori_loop(1, SLOTS // 4, step, 0)
        add(SLOTS // 4 - 1)

    def link_slots():
        lane = lax.broadcasted_iota(jnp.int32, (1, 128), 1)
        live = live_ref[0]
        for index, targets, prev, last in ((row_ref, ROWS, ROW_PREV, ROW_LAST), (col_ref, COLS, COL_PREV, COL_LAST)):
            held = jnp.full((1, 128), -1, jnp.int32)
            for k in range(SLOTS):
                held = jnp.where(lane == k, index[k], held)
            held = jnp.where(lane < live, held, -1)

            def find(match):
                best = jnp.max(jnp.where(match, lane, -1))
                return jnp.where(best < 0, SLOTS, best)

            def before(i, carry):
                for j in range(8):
                    k = i * 8 + j
                    plan[prev + k] = find((held == index[k]) & (lane < k))
                return carry
            lax.fori_loop(0, SLOTS // 8, before, 0)

            def final(i, carry):
                for j in range(8):
                    k = i * 8 + j
                    plan[last + k] = find(held == k)
                return carry
            lax.fori_loop(0, targets // 8, final, 0)

    def link():
        slots[SLOTS] = jnp.zeros(slots.shape[1:], F32)
        link_slots()

    def turn_tiles():
        def turn(k, carry):
            tile = slots[k]
            tiles[k] = jnp.concatenate(split(tile), axis=1)
            tiles_t[k] = jnp.concatenate(split(tile.T), axis=1)
            return carry
        need(load_tiles)
        lax.fori_loop(0, SLOTS, turn, 0, unroll=4)

    def split_features():
        ft_hi[...], ft_lo[...] = split(ft_pad[...])

    def F(h):
        arrive(h, "a5")

        def load(k):
            c = col_ref[k]
            return G[h][c // 16, (c // 4) % 4, (c // 2) % 2, c % 2]
        products(tiles, load, ROW_PREV)
        for i in range(2 * SIDE):
            part[h][i // 2, i % 2] = slots[plan[ROW_LAST + i]]

    def Z1(h):
        for b in range(2):
            for d in (1, 3, 2):
                send(part[h].at[at(z, d), b], zfin[h].at[d - 1, b], dev(dz=d), (h, "z" + str(b)))

    def activate(h, b):
        arrive(h, "z" + str(b))
        need(load_cot)
        rows = pl.ds(b * BLOCK, BLOCK)
        s = (part[h][z, b] + zfin[h][0, b]) + (zfin[h][1, b] + zfin[h][2, b])
        sigma = jax.nn.sigmoid(s)
        act[rows, cols(h)] = s * sigma
        GG[h][z, b] = cot[rows, cols(h)] * sigma * (1.0 + s * (1.0 - sigma))
        own = GG[h].at[z, b]
        for d in (1, 3, 2):
            send(own, own, dev(dz=d), (h, "g" + str(b)))
        store(act.at[rows, cols(h)], act_hbm.at[rows, cols(h)])

    def Z3a(h):
        activate(h, 0)

    def Z3b(h):
        activate(h, 1)

    def B(h):
        arrive(h, "g0")
        arrive(h, "g1")

        def load(k):
            c = row_ref[k]
            return GG[h][c // 2, c % 2]
        products(tiles_t, load, COL_PREV)
        left(h, 0, 1)

        def place(core, b):
            def step(i, carry):
                for j in range(2):
                    k = i * 2 + j
                    G[h][k // 4, k % 4, core, b] = slots[plan[COL_LAST + k * 4 + core * 2 + b]]
                return carry
            lax.fori_loop(0, 8, step, 0)
        for b in range(2):
            place(q, b)
            send(G[h].at[:, :, q, b], R0[h].at[:, :, b], SIB, (h, "s" + str(b)))
        for b in range(2):
            place(p, b)

    def with_own(h, b):
        arrive(h, "s" + str(b))
        s = R0[h]

        def add(i, carry):
            s[i // 4, i % 4, b] = s[i // 4, i % 4, b] + G[h][i // 4, i % 4, p, b]
            return carry
        lax.fori_loop(0, 16, add, 0, unroll=4)

    def R1a(h):
        with_own(h, 0)
        s, m, f = R0[h], m1[h], f1[h]
        send(s.at[xo, :, 0, LO], m.at[0, 0], XR, (h, "m1"))
        send(s.at[xo, :, 0, HI], m.at[0, 1], XL, (h, "m1"))
        send(s.at[xr, :, 0, HI], f.at[0, 0, :, HI], XR, (h, "f1"))
        send(s.at[xl, :, 0, LO], f.at[0, 1, :, LO], XL, (h, "f1"))

    def R1b(h):
        with_own(h, 1)
        s, m, f = R0[h], m1[h], f1[h]
        send(s.at[:, yo, 1, LO], m.at[1, 0], YR, (h, "m1"))
        send(s.at[:, yo, 1, HI], m.at[1, 1], YL, (h, "m1"))
        send(s.at[:, yr, 1, HI], f.at[1, 0, :, HI], YR, (h, "f1"))
        send(s.at[:, yl, 1, LO], f.at[1, 1, :, LO], YL, (h, "f1"))

    def R2(h):
        s, m, f = R0[h], m1[h], f1[h]
        g = (h, "f1")
        arrive(h, "m1")
        s[xr, :, 0, LO] = s[xr, :, 0, LO] + m[0, 0]
        send(s.at[xr, :, 0, LO], f.at[0, 0, :, LO], XR, g)
        s[:, yr, 1, LO] = s[:, yr, 1, LO] + m[1, 0]
        send(s.at[:, yr, 1, LO], f.at[1, 0, :, LO], YR, g)
        s[xl, :, 0, HI] = s[xl, :, 0, HI] + m[0, 1]
        send(s.at[xl, :, 0, HI], f.at[0, 1, :, HI], XL, g)
        s[:, yl, 1, HI] = s[:, yl, 1, HI] + m[1, 1]
        send(s.at[:, yl, 1, HI], f.at[1, 1, :, HI], YL, g)

    def R3(h):
        arrive(h, "f1")
        s, f = R0[h], f1[h]
        f[0, 0] = f[0, 0] + f[0, 1] + s[x, :, 0]
        f[1, 0] = f[1, 0] + f[1, 1] + s[:, y, 1]
        t0, t1, m, b = f.at[0, 0], f.at[1, 0], m2[h], f2[h]
        g = (h, "f2")
        if h == C - 1:
            send(t0.at[yr], b.at[0, 0], YR, g)
            send(t1.at[xr], b.at[1, 0], XR, g)
            send(t0.at[yl], b.at[0, 1], YL, g)
            send(t1.at[xl], b.at[1, 1], XL, g)
            send(t0.at[yo], m.at[0], dev(dy=2), g)
            send(t1.at[xo], m.at[1], dev(dx=2), g)
            return
        send(t0.at[yo, LO], m.at[0, 0], YR, (h, "m2"))
        send(t1.at[xo, LO], m.at[1, 0], XR, (h, "m2"))
        send(t0.at[yo, HI], m.at[0, 1], YL, (h, "m2"))
        send(t1.at[xo, HI], m.at[1, 1], XL, (h, "m2"))
        send(t0.at[yr, HI], b.at[0, 0, HI], YR, g)
        send(t1.at[xr, HI], b.at[1, 0, HI], XR, g)
        send(t0.at[yl, LO], b.at[0, 1, LO], YL, g)
        send(t1.at[xl, LO], b.at[1, 1, LO], XL, g)

    def R4(h):
        if h == C - 1:
            return
        t, m, b = f1[h], m2[h], f2[h]
        arrive(h, "m2")
        for (i, j), rows, target, device in zip(
            ((0, 0), (1, 0), (0, 1), (1, 1)), (LO, LO, HI, HI), (yr, xr, yl, xl), (YR, XR, YL, XL)
        ):
            t[i, 0, target, rows] = t[i, 0, target, rows] + m[i, j]
            send(t.at[i, 0, target, rows], b.at[i, j, rows], device, (h, "f2"))

    def R5(h):
        arrive(h, "f2")
        t, g = f1[h], f2[h]
        own0, own1 = t[0, 0, y] + g[0, 0] + g[0, 1], t[1, 0, x] + g[1, 0] + g[1, 1]
        if h == C - 1:
            own0, own1 = own0 + m2[h][0], own1 + m2[h][1]
        prop[pl.ds(0, BLOCK), cols(h)] = own0
        prop[pl.ds(BLOCK, BLOCK), cols(h)] = own1
        right = split(prop[:, cols(h)])

        def weight_half(core):
            rows = pl.ds(pl.multiple_of(core * (PAD // 2), PAD // 2), PAD // 2)
            gwl[h][core] = mm((ft_hi[rows, :], ft_lo[rows, :]), right)
        weight_half(q)
        send(gwl[h].at[q], sb[h], SIB, (h, "w1"))
        weight_half(p)

    summed = []

    def grad_features(h):
        out = mm_nt(split(w_pad[:, cols(h)]), split(prop[:, cols(h)]))
        summed.append(h)
        if len(summed) == 1:
            gf_acc[...] = out
        else:
            gf_acc[...] = gf_acc[...] + out
        if len(summed) == C:
            gf[...] = gf_acc[pl.ds(0, F_IN), :]
            store(gf, gf_hbm)

    me = dict(x=x, y=y, z=z)

    def peers_of(axis):
        return [(at(me[axis], d), dev(**{"d" + axis: d})) for d in (1, 3, 2)]

    def groups(h):
        if h < C - 1:
            return [(0, PAD // 8, pl.ds(0, PAD // 8), "zxyz")]
        return [(0, 32, pl.ds(0, 32), "zxyz"), (128, 24, pl.ds(32, 24), "yzxy"), (224, 24, pl.ds(56, 24), "xyzx")]

    def piece(first, n, i):
        return pl.ds(pl.multiple_of(first + i * n, 8), n)

    def total(b, part_of):
        return (b[0, part_of] + b[1, part_of]) + (b[2, part_of] + b[3, part_of])

    def W2(h):
        arrive(h, "w1")
        sb[h][...] = sb[h][...] + gwl[h][p]
        for first, n, spot, axes in groups(h):
            mine = me[axes[0]]
            wa[h][mine, spot] = sb[h][piece(first, n, mine)]
            for i, device in peers_of(axes[0]):
                send(sb[h].at[piece(first, n, i)], wa[h].at[mine, spot], device, (h, "w2"))

    def exchange(h, before, after, source, target, step):
        arrive(h, before)
        for first, n, spot, axes in groups(h):
            mine = me[axes[step]]
            target[mine, spot] = total(source, spot)
            own = target.at[mine, spot]
            for i, device in peers_of(axes[step]):
                send(own, own, device, (h, after))

    def W3(h):
        exchange(h, "w2", "w3", wa[h], wb[h], 1)

    def W4(h):
        exchange(h, "w3", "w4", wb[h], wc[h], 2)

    def W5(h):
        arrive(h, "w4")
        for first, n, spot, axes in groups(h):
            rows = piece(first, n, me[axes[3]])
            gwo[h][p, rows] = total(wc[h], spot)
            own = gwo[h].at[p, rows]
            for i, device in peers_of(axes[3]):
                send(own, own, device, (h, "w5"))

    def W6(h):
        arrive(h, "w5")
        own = gwo[h].at[p]
        send(own, own, SIB, (h, "w6"))

    def W7(h):
        arrive(h, "w6")
        half = PAD // 2
        gw[pl.ds(0, half), cols(h)] = gwo[h][0]
        gw[pl.ds(half, F_IN - half), cols(h)] = gwo[h][1, pl.ds(0, F_IN - half)]
        store(gw.at[:, cols(h)], gw_hbm.at[:, cols(h)])

    stages = dict(P=project, A1=A1, A2=A2, A3=A3, A4=A4, A5=A5, F=F, Z1=Z1, Z3a=Z3a, Z3b=Z3b, B=B,
                  R1a=R1a, R1b=R1b, R2=R2, R3=R3, R4=R4, R5=R5, GF=grad_features, W2=W2, W3=W3, W4=W4, W5=W5, W6=W6, W7=W7)

    alone = dict(plan=link, turn=turn_tiles, ft=split_features, drain=drain)
    project(0)
    load_tiles.start()
    load_cot.start()
    pl.semaphore_wait(barrier, len(peers))
    for name in " ".join(ORDER).split()[1:]:
        if name in alone:
            alone[name]()
        else:
            stage, h = name.split("_")
            stages[stage](int(h))
    for h in range(C):
        left(h, 5)
    for copy in stores:
        copy.wait()


ORDER = (
    "P_0 A1_0 P_1 ft",
    "A1_1 P_2 P_3 turn",
    "A2_0 A1_2 A3_0 A2_1",
    "plan A2_2 A4_0 A3_1",
    "A5_0 A1_3 F_0 Z1_0",
    "A4_1 A3_2 Z3a_0 A5_1",
    "A2_3 Z3b_0 F_1 Z1_1",
    "A4_2 A3_3 B_0 Z3a_1",
    "A5_2 Z3b_1 F_2 Z1_2",
    "A4_3 R1b_0 R1a_0 B_1",
    "A5_3 Z3a_2 Z3b_2 R2_0",
    "R1a_1 R1b_1 F_3 Z1_3",
    "B_2 R3_0 R2_1 Z3a_3",
    "Z3b_3 R4_0 R1a_2 R1b_2",
    "R3_1 R5_0 B_3 R2_2",
    "W2_0 R4_1 GF_0 R1a_3",
    "R1b_3 R3_2 R5_1 GF_1",
    "W2_1 R2_3 W3_0 R4_2",
    "R3_3 W3_1 R5_2 W4_0",
    "W2_2 R5_3 W2_3 W3_2",
    "W4_1 W5_0 GF_2 W3_3",
    "W4_2 W5_1 drain W4_3",
    "W5_2 W6_1 GF_3 R4_3",
    "W5_3 W7_1 W6_2 W6_0",
    "W6_3 W7_2 W7_0 W7_3",
)


def hand_over(*refs):
    arrays, results, held, load_sem, store_sem = refs[:3], refs[3:6], refs[6:9], refs[9], refs[10]
    pieces = []
    for i, axis in ((2, 1), (1, 1), (0, 0)):
        size = arrays[i].shape[axis] // 2
        for j in range(2):
            part = pl.ds(j * size, size)
            pieces.append((i, (slice(None), part) if axis else (part, slice(None))))
    loads = [
        pltpu.make_async_copy(arrays[i].at[place], held[i].at[place], load_sem.at[n])
        for n, (i, place) in enumerate(pieces)]
    stores = [
        pltpu.make_async_copy(held[i].at[place], results[i].at[place], store_sem.at[n])
        for n, (i, place) in enumerate(pieces)]
    for load in loads:
        load.start()
    for load, store in zip(loads, stores):
        load.wait()
        store.start()
    for store in stores:
        store.wait()


def body(features, weight, cotangent, tile_values, tile_row, tile_col, tile_count):
    hidden = weight.shape[1]
    nodes, width = features.shape
    C = CHUNKS
    W = hidden // C

    def vmem(*shape, dtype=F32, count=C):
        return [pltpu.VMEM(shape, dtype)] * count

    scratch = (
        vmem(4, 4, 2, 2, BLOCK, W)
        + vmem(4, 4, 2, BLOCK, W)
        + vmem(4, 2, BLOCK, W)
        + vmem(3, 2, BLOCK, W)
        + vmem(4, 2, BLOCK, W)
        + vmem(2, 2, 4, HALF, W)
        + vmem(2, 2, 4, BLOCK, W)
        + vmem(2, 2, HALF, W, count=C - 1)
        + vmem(2, BLOCK, W, count=1)
        + vmem(2, 2, BLOCK, W)
        + vmem(2, PAD // 2, W)
        + vmem(PAD // 2, W)
        + vmem(4, PAD // 8, W)
        + vmem(4, PAD // 8, W)
        + vmem(4, PAD // 8, W)
        + vmem(2, PAD // 2, W)
        + [
            pltpu.VMEM((SLOTS + 1, BLOCK, W), F32),
            pltpu.VMEM((SLOTS, BLOCK, 2 * BLOCK), BF16),
            pltpu.VMEM((SLOTS, BLOCK, 2 * BLOCK), BF16),
            pltpu.VMEM((width, hidden), F32),
            pltpu.VMEM((PAD, hidden), F32),
            pltpu.VMEM((width, nodes), F32),
            pltpu.VMEM((nodes, hidden), F32),
            pltpu.VMEM((nodes, PAD), BF16),
            pltpu.VMEM((nodes, PAD), BF16),
            pltpu.VMEM((PAD, nodes), BF16),
            pltpu.VMEM((PAD, nodes), BF16),
            pltpu.VMEM((nodes, hidden), F32),
            pltpu.VMEM((PAD, nodes), F32),
            pltpu.SMEM((2 * SLOTS + ROWS + COLS,), jnp.int32),
            pltpu.VMEM((nodes, hidden), F32),
            pltpu.VMEM((width, nodes), F32),
            pltpu.VMEM((width, hidden), F32),
            pltpu.SemaphoreType.DMA((len(POOLS) * C,)),
            pltpu.SemaphoreType.DMA((GROUPS * C,)),
            pltpu.SemaphoreType.DMA((3 + C,)),
            pltpu.SemaphoreType.DMA((3 * C + 1,)),
        ]
    )
    scalars = pl.BlockSpec(memory_space=pltpu.SMEM)
    hbm = pl.BlockSpec(memory_space=pl.ANY)
    shapes = (
        jax.ShapeDtypeStruct((nodes, hidden), F32),
        jax.ShapeDtypeStruct((width, nodes), F32),
        jax.ShapeDtypeStruct((width, hidden), F32),
    )
    results = pl.pallas_call(
        kernel,
        out_shape=shapes,
        in_specs=[scalars] * 3 + [hbm] * 4,
        out_specs=(hbm, hbm, hbm),
        scratch_shapes=scratch,
        compiler_params=pltpu.CompilerParams(
            collective_id=0, has_side_effects=True, vmem_limit_bytes=62 * 1024 * 1024),
    )(tile_row, tile_col, tile_count, features.T, weight, cotangent, tile_values)
    activated, grad_features, grad_weight = pl.pallas_call(
        hand_over,
        out_shape=shapes,
        in_specs=[hbm] * 3,
        out_specs=(hbm,) * 3,
        scratch_shapes=[pltpu.VMEM(shape.shape, F32) for shape in shapes] + [pltpu.SemaphoreType.DMA((6,))] * 2,
        compiler_params=pltpu.CompilerParams(vmem_limit_bytes=62 * 1024 * 1024),
    )(*results)
    return activated, grad_features.T, grad_weight


def solution(mesh):
    in_specs = (
        P(("rows", "rep"), None),
        P(),
        P(("rows", "rep"), None),
        P(("rows", "rep"), None, None),
        P(("rows", "rep")),
        P(("rows", "rep")),
        P(("rows", "rep")),
    )
    out_specs = (P(("rows", "rep"), None), P(("rows", "rep"), None), P())
    return jax.shard_map(body, mesh=mesh, in_specs=in_specs, out_specs=out_specs, check_vma=False)
```
